32 devices in a mesh: blk: 8 (over z, x), seq: 4 (over y, core).
Axes of the slice: x: 2, y: 2, z: 4, core: 2. Of those that a mesh axis runs over, the one named last changes fastest.
Arguments:
- signal: float32 [32768, 512], P(('blk', 'seq')), may hold values from -6 to 6
- item_start: int32 [32768], P(('blk', 'seq')), may hold values from 0 to 31680, as said below
- frame_slot: int32 [32768], P(('blk', 'seq')), may hold values from 0 to 221, as said below
- mel_frames: float32 [224, 80], P(('blk', 'seq')), may hold values from -6 to 6
- resid_cotan: float32 [32768, 512], P(('blk', 'seq')), may hold values from -6 to 6
- skip_cotan: float32 [32768, 512], P(('blk', 'seq')), may hold values from -6 to 6
- conv_weight: float32 [2, 512, 1024], replicated, may hold values from -0.1875 to 0.1875
- cond_weight: float32 [80, 1024], replicated, may hold values from -0.625 to 0.625
- proj_weight: float32 [512, 1024], replicated, may hold values from -0.75 to 0.75
- biases: float32 [2048], replicated, may hold values from -4 to 4
- conv_moment: float32 [2, 512, 1024], replicated, may hold values from -1792 to 1792
- cond_moment: float32 [80, 1024], replicated, may hold values from -1792 to 1792
- proj_moment: float32 [512, 1024], replicated, may hold values from -384 to 384
- biases_moment: float32 [2048], replicated, may hold values from -1280 to 1280
- conv_average: float32 [2, 512, 1024], replicated, may hold values from -0.1875 to 0.1875
- cond_average: float32 [80, 1024], replicated, may hold values from -0.625 to 0.625
- proj_average: float32 [512, 1024], replicated, may hold values from -0.75 to 0.75
- biases_average: float32 [2048], replicated, may hold values from -4 to 4
Outputs:
- residual: float32 [32768, 512], P(('blk', 'seq'))
- skip_out: float32 [32768, 512], P(('blk', 'seq'))
- signal_grad: float32 [32768, 512], P(('blk', 'seq'))
- mel_grad: float32 [224, 80], P(('blk', 'seq'))
- conv_updated: float32 [2, 512, 1024], replicated
- cond_updated: float32 [80, 1024], replicated
- proj_updated: float32 [512, 1024], replicated
- biases_updated: float32 [2048], replicated
- conv_moment_new: float32 [2, 512, 1024], replicated
- cond_moment_new: float32 [80, 1024], replicated
- proj_moment_new: float32 [512, 1024], replicated
- biases_moment_new: float32 [2048], replicated
- conv_average_new: float32 [2, 512, 1024], replicated
- cond_average_new: float32 [80, 1024], replicated
- proj_average_new: float32 [512, 1024], replicated
- biases_average_new: float32 [2048], replicated
- conv_copy: bfloat16 [2, 512, 1024], replicated
- cond_copy: bfloat16 [80, 1024], replicated
- proj_copy: bfloat16 [512, 1024], replicated
- biases_copy: bfloat16 [2048], replicated
The draws below stay inside these ranges and needn't reach their ends.
Inputs may be any that keep to these rules, and one draw needn't show every extreme that they name: `item_start`: each clip holds a whole number of mel frames of 200 or 300 samples and at least 1024 samples, except the last two clips, which may be cut short; the last clip begins at sample 32768 - 1088 with frames of 200 samples. This is the first sample of the sample's clip. `frame_slot`: frames are stored 7 slots to each block of 1024 samples, in the block that holds the frame's first sample, in order of time; a sample's frame lies in the sample's own block or in the block before it. Slots that no sample names hold unused values.
All inputs are finite; a program needn't handle non-finite values.
Results may differ from the reference program's by a relative error of at most 0.001.
Values sent between devices are 32-bit elements; how exact they have to be, the bound alone decides.
No kernel may reach another device: no remote copies, remote signals or barrier semaphores. Data moves between devices by JAX's collectives and lax.ppermute only.
A program may use at most 128 MiB of HBM per device.

```python
import math
import jax
import jax.numpy as jnp
from jax import lax

RESID = 512
GATE = 1024
SKIPS = 512
MELS = 80
DILATION = 64
HOP_LOW = 200
HOP_HIGH = 300
TOK_DEV = 1024
FR_DEV = 7
TOKENS = 32768
FRAMES = 224


def clip_layout(key):
    item_count = TOKENS // TOK_DEV + 1
    first_key, second_key = jax.random.split(key)
    picked = jax.random.randint(first_key, (item_count,), 0, 2)
    hop_drawn = jnp.where(picked == 0, HOP_LOW, HOP_HIGH).astype(jnp.int32)
    least = (TOK_DEV + hop_drawn - 1) // hop_drawn
    spread = 4 * ((TOK_DEV + HOP_LOW - 1) // HOP_LOW)
    extra = jax.random.randint(second_key, (item_count,), 0, spread)
    length = (least + extra).astype(jnp.int32) * hop_drawn
    ending_drawn = jnp.cumsum(length).astype(jnp.int32)
    begins_drawn = ending_drawn - length
    cut_point = TOKENS - TOK_DEV - DILATION
    item_ids = jnp.arange(item_count, dtype=jnp.int32)
    last_kept = jnp.searchsorted(ending_drawn, cut_point, side='right').astype(jnp.int32)
    far_away = 2 * TOKENS + item_ids
    begins = jnp.where(item_ids <= last_kept, begins_drawn, jnp.where(item_ids == last_kept + 1, cut_point, far_away)).astype(jnp.int32)
    ending = jnp.where(item_ids < last_kept, ending_drawn, jnp.where(item_ids == last_kept, cut_point, jnp.where(item_ids == last_kept + 1, TOKENS, far_away))).astype(jnp.int32)
    hop_size = jnp.where(item_ids == last_kept + 1, HOP_LOW, hop_drawn).astype(jnp.int32)
    frame_count = (ending - begins + hop_size - 1) // hop_size
    frames_before = (jnp.cumsum(frame_count) - frame_count).astype(jnp.int32)
    sample_time = jnp.arange(TOKENS, dtype=jnp.int32)
    item_index = jnp.searchsorted(ending, sample_time, side='right').astype(jnp.int32)
    start_of = begins[item_index]
    hop_of = hop_size[item_index]
    within_item = (sample_time - start_of) // hop_of
    first_sample = start_of + within_item * hop_of
    owner = first_sample // TOK_DEV
    block_base = owner * TOK_DEV
    base_item = jnp.minimum(jnp.searchsorted(ending, block_base, side='right').astype(jnp.int32), item_count - 1)
    base_count = frames_before[base_item] + jnp.maximum(block_base - begins[base_item] + hop_size[base_item] - 1, 0) // hop_size[base_item]
    own_count = frames_before[item_index] + within_item
    slot_of = owner * FR_DEV + own_count - base_count
    return (start_of.astype(jnp.int32), slot_of.astype(jnp.int32))


def draw_item_start(key, part):
    start_of, slot_of = clip_layout(key)
    return start_of


def draw_frame_slot(key, part):
    start_of, slot_of = clip_layout(key)
    return slot_of


def levels(own_key, dims, shards, smallest, largest):
    def one(position, blocks):
        heights = jax.random.uniform(jax.random.fold_in(jax.random.fold_in(own_key, 6), position), (blocks,), jnp.float32, smallest / len(shards), largest / len(shards))
        return jnp.repeat(jnp.exp(heights), dims[position] // blocks).reshape((-1,) + (1,) * (len(dims) - position - 1))

    gain = one(*shards[0])
    for cut in shards[1:]:
        gain = gain * one(*cut)
    return gain


def centred(own_key, extent, width, most, cuts=(), held_as=jnp.bfloat16):
    gain = levels(own_key, extent, cuts, -0.22, 0.18) if cuts else 1.0
    result = jax.random.normal(own_key, extent, jnp.float32) * width * gain
    return jnp.minimum(jnp.maximum(result, -most), most).astype(held_as)


def setup_inputs(seed: int = 0) -> dict:
    seeds = jax.random.split(jax.random.key(seed), 19)
    signal = centred(seeds[0], (TOKENS, RESID), 1.0, 6.0, ((0, 32),), jnp.float32)
    item_start = draw_item_start(jax.random.fold_in(seeds[18], 71), 0)
    frame_slot = draw_frame_slot(jax.random.fold_in(seeds[18], 71), 0)
    mel_frames = centred(seeds[3], (FRAMES, MELS), 1.0, 6.0, ((0, 32),), jnp.float32)
    resid_cotan = centred(seeds[4], (TOKENS, RESID), 1.0, 6.0, ((0, 32),), jnp.float32)
    skip_cotan = centred(seeds[5], (TOKENS, SKIPS), 1.0, 6.0, ((0, 32),), jnp.float32)
    conv_weight = centred(seeds[6], (2, RESID, GATE), (2 * RESID) ** -0.5, 0.1875, (), jnp.float32)
    cond_weight = centred(seeds[7], (MELS, GATE), MELS ** -0.5, 0.625, (), jnp.float32)
    proj_weight = centred(seeds[8], (GATE // 2, RESID + SKIPS), (GATE // 16) ** -0.5, 0.75, (), jnp.float32)
    biases = centred(seeds[9], (GATE + RESID + SKIPS,), 0.3, 4.0, (), jnp.float32)
    conv_moment = centred(seeds[10], (2, RESID, GATE), (1.6 * TOKENS ** 0.5), 1792.0, (), jnp.float32)
    cond_moment = centred(seeds[11], (MELS, GATE), (1.6 * TOKENS ** 0.5), 1792.0, (), jnp.float32)
    proj_moment = centred(seeds[12], (GATE // 2, RESID + SKIPS), (0.35 * TOKENS ** 0.5), 384.0, (), jnp.float32)
    biases_moment = centred(seeds[13], (GATE + RESID + SKIPS,), (1.3 * TOKENS ** 0.5), 1280.0, (), jnp.float32)
    conv_average = centred(seeds[14], (2, RESID, GATE), (2 * RESID) ** -0.5, 0.1875, (), jnp.float32)
    cond_average = centred(seeds[15], (MELS, GATE), MELS ** -0.5, 0.625, (), jnp.float32)
    proj_average = centred(seeds[16], (GATE // 2, RESID + SKIPS), (GATE // 16) ** -0.5, 0.75, (), jnp.float32)
    biases_average = centred(seeds[17], (GATE + RESID + SKIPS,), 0.3, 4.0, (), jnp.float32)
    return dict(signal=signal, item_start=item_start, frame_slot=frame_slot, mel_frames=mel_frames, resid_cotan=resid_cotan, skip_cotan=skip_cotan, conv_weight=conv_weight, cond_weight=cond_weight, proj_weight=proj_weight, biases=biases, conv_moment=conv_moment, cond_moment=cond_moment, proj_moment=proj_moment, biases_moment=biases_moment, conv_average=conv_average, cond_average=cond_average, proj_average=proj_average, biases_average=biases_average)


@jax.custom_vjp
def low(v):
    return lax.optimization_barrier(v.astype(jnp.bfloat16)).astype(jnp.float32)

@jax.custom_vjp
def low_back(v):
    return v

def low_keep(v):
    return (low(v), None)

def low_pass(kept, grad):
    return (grad,)

def back_keep(v):
    return (v, None)

def back_low(kept, grad):
    return (low(grad),)
low.defvjp(low_keep, low_pass)
low_back.defvjp(back_keep, back_low)
highest = lax.Precision.HIGHEST
momentum_rate = 0.9
ema_decay = 0.5
step_scale = 0.15

def matmul(left, right):
    return jnp.dot(left, right, precision=highest, preferred_element_type=jnp.float32)

def forward(signal, mel_frames, conv_weight, cond_weight, proj_weight, biases, item_start, frame_slot):
    sample_time = jnp.arange(signal.shape[0], dtype=jnp.int32)
    usable = (sample_time - DILATION >= item_start).astype(jnp.float32)[:, None]
    delayed = jnp.concatenate([jnp.zeros((DILATION, RESID), jnp.float32), signal[:-DILATION]], 0) * usable
    conditioning = jnp.take(mel_frames, frame_slot, axis=0)
    preact = matmul(delayed, conv_weight[0]) + matmul(signal, conv_weight[1]) + matmul(conditioning, cond_weight) + biases[:GATE]
    half_gate = GATE // 2
    gated_out = jnp.tanh(preact[:, :half_gate]) * jax.nn.sigmoid(preact[:, half_gate:])
    mixed_out = matmul(gated_out, proj_weight) + biases[GATE:]
    return (signal + mixed_out[:, :RESID], mixed_out[:, RESID:])

def update(weight, gradient, moment, average, step_rate):
    moment_new = momentum_rate * moment + gradient
    weight_new = weight - step_rate * (gradient + momentum_rate * moment_new)
    average_new = ema_decay * average + (1.0 - ema_decay) * weight_new
    return (weight_new, moment_new, average_new, weight_new.astype(jnp.bfloat16))

def reference(signal, item_start, frame_slot, mel_frames, resid_cotan, skip_cotan, conv_weight, cond_weight, proj_weight, biases, conv_moment, cond_moment, proj_moment, biases_moment, conv_average, cond_average, proj_average, biases_average):

    def closed(signal, mel_frames, conv_weight, cond_weight, proj_weight, biases):
        return forward(signal, mel_frames, conv_weight, cond_weight, proj_weight, biases, item_start, frame_slot)
    outputs, pullback = jax.vjp(closed, signal, mel_frames, conv_weight, cond_weight, proj_weight, biases)
    residual, skip_out = outputs
    signal_grad, mel_grad, conv_grad, cond_grad, proj_grad, biases_grad = pullback((resid_cotan, skip_cotan))
    root = math.sqrt(TOKENS)
    conv_rate = step_scale / (math.sqrt(2 * RESID) * 1.5 * root)
    cond_rate = step_scale / (math.sqrt(MELS) * 1.5 * root)
    proj_rate = step_scale / (math.sqrt(GATE // 16) * 0.3 * root)
    biases_rate = step_scale * 0.3 / (1.2 * root)
    conv_a, conv_b, conv_c, conv_d = update(conv_weight, conv_grad, conv_moment, conv_average, conv_rate)
    cond_a, cond_b, cond_c, cond_d = update(cond_weight, cond_grad, cond_moment, cond_average, cond_rate)
    proj_a, proj_b, proj_c, proj_d = update(proj_weight, proj_grad, proj_moment, proj_average, proj_rate)
    bias_a, bias_b, bias_c, bias_d = update(biases, biases_grad, biases_moment, biases_average, biases_rate)
    return (residual, skip_out, signal_grad, mel_grad, conv_a, cond_a, proj_a, bias_a, conv_b, cond_b, proj_b, bias_b, conv_c, cond_c, proj_c, bias_c, conv_d, cond_d, proj_d, bias_d)
```

```python
import math

import jax
import jax.numpy as jnp
from jax import lax
from jax.sharding import PartitionSpec as P

RESID = 512
GATE = 1024
MELS = 80
DILATION = 64


highest = lax.Precision.HIGHEST
momentum_rate = 0.9
ema_decay = 0.5
step_scale = 0.15


def from_behind(x, axis, by):
    count = lax.axis_size(axis)
    pairs = [(i, i + by) for i in range(count) if 0 <= i + by < count]
    return lax.ppermute(x, axis, pairs)


def matmul(left, right):
    return jnp.dot(left, right, precision=lax.Precision.HIGH, preferred_element_type=jnp.float32)


def plan(blk, seq):
    if (blk, seq) == (8, 4):
        return 0, ((2, 1, 3, 4), (1, 2, 4, 3))
    count = (blk * seq).bit_length() - 1
    if (blk, seq) == (64, 4):
        return 2, ((6, 0, 3, 7, 1, 4, 5), (0, 6, 3, 1, 7, 4, 5))
    rest = tuple(range(1, count))
    return 0, (rest, rest)


class Tree:
    def __init__(self):
        blk, seq = lax.axis_size("blk"), lax.axis_size("seq")
        self.count = blk * seq
        core_bit, (first, second) = plan(blk, seq)
        me = lax.axis_index(("blk", "seq"))
        core = (me >> core_bit) & 1
        self.bits = [core]
        self.pairs = [[(i, i ^ (1 << core_bit)) for i in range(self.count)]]
        for a, b in zip(first, second):
            self.bits.append(jnp.where(core == 0, (me >> a) & 1, (me >> b) & 1))
            self.pairs.append(
                [(i, i ^ (1 << (b if (i >> core_bit) & 1 else a))) for i in range(self.count)]
            )

    def swap(self, x, step):
        return lax.ppermute(x, ("blk", "seq"), self.pairs[step])

    def scatter(self, x):
        def half(y, which):
            size = y.shape[0] // 2
            return lax.dynamic_slice_in_dim(y, which * size, size, 0)

        bit = self.bits[0]
        send, keep = half(x, 1 - bit), half(x, bit)
        for step in range(len(self.bits)):
            got = self.swap(send, step)
            if step + 1 == len(self.bits):
                return keep + got
            bit = self.bits[step + 1]
            send = half(keep, 1 - bit) + half(got, 1 - bit)
            keep = half(keep, bit) + half(got, bit)

    def gather(self, x):
        for step in reversed(range(len(self.bits))):
            got = self.swap(x, step)
            x = jnp.where(
                self.bits[step] == 0, jnp.concatenate([x, got]), jnp.concatenate([got, x])
            )
        return x

    def total(self, x):
        return self.gather(self.scatter(x))


def to_tiles(x):
    rows = x.shape[0]
    return x.reshape(rows // 8, 8, 8, 128).transpose(0, 2, 1, 3).reshape(rows, 8, 128)


def from_tiles(x):
    rows = x.shape[0]
    return x.reshape(rows // 8, 8, 8, 128).transpose(0, 2, 1, 3).reshape(rows, 1024)


def update(weight, gradient, moment, average, step_rate):
    moment_new = momentum_rate * moment + gradient
    weight_new = weight - step_rate * (gradient + momentum_rate * moment_new)
    average_new = ema_decay * average + (1.0 - ema_decay) * weight_new
    return (weight_new, moment_new, average_new, weight_new.astype(jnp.bfloat16))


def shards(
    signal,
    item_start,
    frame_slot,
    mel_frames,
    resid_cotan,
    skip_cotan,
    conv_weight,
    cond_weight,
    proj_weight,
    biases,
    conv_moment,
    cond_moment,
    proj_moment,
    biases_moment,
    conv_average,
    cond_average,
    proj_average,
    biases_average,
):
    row_count, res_width = signal.shape
    slot_count = mel_frames.shape[0]
    half_gate = GATE // 2
    position = lax.axis_index(("blk", "seq"))
    sample_time = position * row_count + jnp.arange(row_count, dtype=jnp.int32)
    usable = (sample_time - DILATION >= item_start).astype(jnp.float32)[:, None]
    tail_rows, prior_frames = from_behind(
        (signal[row_count - DILATION :], mel_frames), ("blk", "seq"), 1
    )
    delayed = jnp.concatenate([tail_rows, signal[: row_count - DILATION]], 0) * usable
    frames = jnp.concatenate([prior_frames, mel_frames], 0)
    local_slot = frame_slot - (position - 1) * slot_count
    select = (local_slot[:, None] == jnp.arange(2 * slot_count, dtype=jnp.int32)[None, :]).astype(
        jnp.float32
    )
    projected = matmul(frames, cond_weight)
    preact = (
        matmul(delayed, conv_weight[0])
        + matmul(signal, conv_weight[1])
        + matmul(select, projected)
        + biases[:GATE]
    )
    tanh_part = jnp.tanh(preact[:, :half_gate])
    sigm_part = jax.nn.sigmoid(preact[:, half_gate:])
    gated_out = tanh_part * sigm_part
    mixed_out = matmul(gated_out, proj_weight) + biases[GATE:]
    residual = signal + mixed_out[:, :res_width]
    skip_out = mixed_out[:, res_width:]
    upstream = jnp.concatenate([resid_cotan, skip_cotan], 1)
    proj_grad = matmul(gated_out.T, upstream)
    grad_gated = matmul(upstream, proj_weight.T)
    grad_pre = jnp.concatenate(
        [
            grad_gated * sigm_part * (1.0 - tanh_part * tanh_part),
            grad_gated * tanh_part * sigm_part * (1.0 - sigm_part),
        ],
        1,
    )
    biases_grad = jnp.concatenate([jnp.sum(grad_pre, 0), jnp.sum(upstream, 0)])
    conv_grad = jnp.stack([matmul(delayed.T, grad_pre), matmul(signal.T, grad_pre)])
    grad_frames = matmul(select.T, grad_pre)
    cond_grad = matmul(frames.T, grad_frames)
    grad_mel_all = matmul(grad_frames, cond_weight.T)
    grad_delayed = matmul(grad_pre, conv_weight[0].T) * usable
    back_rows, back_frames = from_behind(
        (grad_delayed[:DILATION], grad_mel_all[:slot_count]), ("blk", "seq"), -1
    )
    filler = jnp.zeros((DILATION, res_width), jnp.float32)
    signal_grad = (
        resid_cotan
        + matmul(grad_pre, conv_weight[1].T)
        + jnp.concatenate([grad_delayed[DILATION:], filler], 0)
        + jnp.concatenate([jnp.zeros((row_count - DILATION, res_width), jnp.float32), back_rows], 0)
    )
    mel_grad = grad_mel_all[slot_count:] + back_frames
    tree = Tree()
    proj_grad = tree.total(proj_grad)
    first_grad = tree.total(conv_grad[0])
    few = MELS + 2
    spare = -few % tree.count
    second = jnp.concatenate(
        [
            to_tiles(conv_grad[1]),
            cond_grad.reshape(MELS, 8, 128),
            biases_grad.reshape(2, 8, 128),
            jnp.zeros((spare, 8, 128), jnp.float32),
        ]
    )
    second = tree.total(second)
    conv_grad = jnp.stack([first_grad, from_tiles(second[:RESID])])
    cond_grad = second[RESID : RESID + MELS].reshape(MELS, GATE)
    biases_grad = second[RESID + MELS : RESID + few].reshape(-1)
    tokens = row_count * lax.axis_size("blk") * lax.axis_size("seq")
    root = math.sqrt(tokens)
    conv_rate = step_scale / (math.sqrt(2 * RESID) * 1.5 * root)
    cond_rate = step_scale / (math.sqrt(MELS) * 1.5 * root)
    proj_rate = step_scale / (math.sqrt(GATE // 16) * 0.3 * root)
    biases_rate = step_scale * 0.3 / (1.2 * root)
    conv_a, conv_b, conv_c, conv_d = update(
        conv_weight, conv_grad, conv_moment, conv_average, conv_rate
    )
    cond_a, cond_b, cond_c, cond_d = update(
        cond_weight, cond_grad, cond_moment, cond_average, cond_rate
    )
    proj_a, proj_b, proj_c, proj_d = update(
        proj_weight, proj_grad, proj_moment, proj_average, proj_rate
    )
    bias_a, bias_b, bias_c, bias_d = update(
        biases, biases_grad, biases_moment, biases_average, biases_rate
    )
    return (
        residual,
        skip_out,
        signal_grad,
        mel_grad,
        conv_a,
        cond_a,
        proj_a,
        bias_a,
        conv_b,
        cond_b,
        proj_b,
        bias_b,
        conv_c,
        cond_c,
        proj_c,
        bias_c,
        conv_d,
        cond_d,
        proj_d,
        bias_d,
    )


def solution(mesh):
    in_specs = (
        P(("blk", "seq"), None),
        P(("blk", "seq")),
        P(("blk", "seq")),
        P(("blk", "seq"), None),
        P(("blk", "seq"), None),
        P(("blk", "seq"), None),
        P(),
        P(),
        P(),
        P(),
        P(),
        P(),
        P(),
        P(),
        P(),
        P(),
        P(),
        P(),
    )
    out_specs = (
        P(("blk", "seq"), None),
        P(("blk", "seq"), None),
        P(("blk", "seq"), None),
        P(("blk", "seq"), None),
        P(),
        P(),
        P(),
        P(),
        P(),
        P(),
        P(),
        P(),
        P(),
        P(),
        P(),
        P(),
        P(),
        P(),
        P(),
        P(),
    )
    return jax.shard_map(shards, mesh=mesh, in_specs=in_specs, out_specs=out_specs, check_vma=False)
```

```python
import math

import jax
import jax.numpy as jnp
from jax import lax
from jax.experimental import pallas as pl
from jax.experimental.pallas import tpu as pltpu
from jax.sharding import PartitionSpec as P

RESID = 512
GATE = 1024
MELS = 80
DILATION = 64
HALF = 512

f32 = jnp.float32
bf16 = jnp.bfloat16
momentum_rate = 0.9
ema_decay = 0.5
step_scale = 0.15
axes = ("blk", "seq")

VMEM = pl.BlockSpec(memory_space=pltpu.VMEM)
HBM = pl.BlockSpec(memory_space=pltpu.HBM)
ANY = pl.BlockSpec(memory_space=pl.ANY)
MIB = 1 << 20


TOKEN = ((8, 128), f32)

RATE = 3e9
TIMES = {
    "pack": 1, "late_gates": 8, "early_gates": 6, "proj_grad_send": 1.8, "gate_grad": 5.8,
    "tap0_send": 1.8, "tap0_keep_tap1_send": 4.5, "tap1_keep": 1.8, "mix": 2.8, "signal_grad": 4.4,
    "back": 1.4, "few_update": 1.2, "update": 2,
}
FOLD = 0.1


def expected(name):
    for key in sorted(TIMES, key=len, reverse=True):
        if key in name:
            return TIMES[key]
    return FOLD


class Order:
    def __init__(self):
        self.last = None

    def call(
        self, body, name, ins, outs, specs=None, out_specs=None, scratch=(), limit=16, aliases=None
    ):
        specs = list(specs) if specs else [VMEM] * len(ins)
        ins = [
            pltpu.with_memory_space_constraint(x, pltpu.HBM) if s is HBM else x
            for x, s in zip(ins, specs)
        ]
        out_specs = list(out_specs) if out_specs else [VMEM] * len(outs)
        after = [] if self.last is None else [self.last]
        n_in, n_after, n_out = len(ins), len(after), len(outs)

        def run(*refs):
            outs = refs[n_in + n_after : n_in + n_after + n_out]
            token = refs[n_in + n_after + n_out]
            token[...] = jnp.zeros(token.shape, f32)
            body(*refs[:n_in], *outs, *refs[n_in + n_after + n_out + 1 :])

        kinds = {id(VMEM): pltpu.VMEM, id(HBM): pltpu.HBM}
        *result, self.last = pl.pallas_call(
            run,
            out_shape=[kinds[id(s)](*o) for o, s in zip(outs, out_specs)] + [pltpu.VMEM(*TOKEN)],
            in_specs=specs + [VMEM] * n_after,
            out_specs=out_specs + [VMEM],
            scratch_shapes=list(scratch),
            input_output_aliases=aliases or {},
            compiler_params=pltpu.CompilerParams(vmem_limit_bytes=limit * MIB),
            cost_estimate=pl.CostEstimate(
                flops=int(RATE * expected(name)), bytes_accessed=1, transcendentals=0
            ),
            name=name,
        )(*ins, *after)
        return result


def split(x):
    high = x.astype(bf16)
    return high, (x - high.astype(f32)).astype(bf16)


def dot(left, right, over):
    return lax.dot_general(left, right, (over, ((), ())), preferred_element_type=f32)


def exact(left, right, over):
    return lax.dot_general(
        left, right, (over, ((), ())), preferred_element_type=f32, precision=lax.Precision.HIGHEST
    )


NN = ((1,), (0,))
NT = ((1,), (1,))
TN = ((0,), (0,))


def plan(blk, seq):
    if (blk, seq) == (8, 4):
        return 0, ((2, 1, 3, 4), (1, 2, 4, 3))
    if (blk, seq) == (64, 4):
        return 2, ((6, 0, 3, 7, 1, 4, 5), (0, 6, 3, 1, 7, 4, 5))
    count = (blk * seq).bit_length() - 1
    rest = tuple(range(1, count))
    return 0, (rest, rest)


class Pairs:
    def __init__(self):
        blk, seq = lax.axis_size("blk"), lax.axis_size("seq")
        self.count = blk * seq
        self.core_bit, (first, second) = plan(blk, seq)
        self.places = [(self.core_bit, self.core_bit), *zip(first, second)]
        self.steps = len(self.places)
        self.pairs = [
            [(i, i ^ (1 << p[(i >> self.core_bit) & 1])) for i in range(self.count)]
            for p in self.places
        ]

    def bit(self, step, sibling=False):
        me = lax.axis_index(axes)
        core = (me >> self.core_bit) & 1
        if sibling:
            core = 1 - core
        if step == 0:
            return core
        a, b = self.places[step]
        return jnp.where(core == 0, (me >> a) & 1, (me >> b) & 1)

    def swap(self, x, step):
        return lax.ppermute(x, axes, self.pairs[step])


class Sum:
    def __init__(self, order, pairs, name, send, whole=1):
        self.order, self.pairs, self.name = order, pairs, name
        self.parted = pairs.steps - whole
        self.step, self.back = 0, False
        self.got = pairs.swap(send, 0)
        self.done = False

    def advance(self):
        if self.done:
            return
        pairs, step = self.pairs, self.step
        label = f"{self.name}_{'join' if self.back else 'fold'}{step}"
        if self.back:
            size = self.piece.shape[0]

            def body(mine, got, out):
                bit = pairs.bit(step)
                out[pl.ds(bit * size, size)] = mine[...]
                out[pl.ds((1 - bit) * size, size)] = got[...]

            (self.piece,) = self.order.call(
                body, label, [self.piece, self.got], [((2 * size, 8, 128), f32)]
            )
            self.step -= 1
        elif step + 1 < self.parted:
            half = self.rest.shape[0] // 2

            def body(keep, got, send, rest):
                bit = pairs.bit(step + 1)
                here, there = pl.ds(bit * half, half), pl.ds((1 - bit) * half, half)
                send[...] = keep[there] + got[there]
                rest[...] = keep[here] + got[here]

            shape = ((half, 8, 128), f32)
            send, self.rest = self.order.call(body, label, [self.rest, self.got], [shape, shape])
            self.step += 1
            self.got = pairs.swap(send, self.step)
            return
        else:
            mine = self.rest if step < self.parted else self.piece

            def body(mine, got, out):
                out[...] = mine[...] + got[...]

            (self.piece,) = self.order.call(body, label, [mine, self.got], [(mine.shape, f32)])
            self.step += 1
            if self.step == pairs.steps:
                self.back, self.step = True, self.parted - 1
        if self.back and self.step == 1:
            self.done = True
            return
        self.got = pairs.swap(self.piece, self.step)


def pack_body(rows, signal, mel, out, frames, sem):
    copy = pltpu.make_async_copy(
        signal.at[pl.ds(rows - DILATION, DILATION)], out.at[pl.ds(0, DILATION)], sem.at[0]
    )
    other = pltpu.make_async_copy(mel, frames, sem.at[1])
    copy.start()
    other.start()
    out[DILATION:, :] = jnp.zeros((8, RESID), f32)
    other.wait()
    out[DILATION : DILATION + mel.shape[0], :MELS] = frames[...]
    copy.wait()


def columns(row, rows):
    return jnp.transpose(jnp.broadcast_to(row, (8, rows)))[:, :1]


def picks(slots, part, slot_count, sel):
    me = lax.axis_index(axes)
    local = (slots[:, part * HALF : (part + 1) * HALF] - (me - 1) * slot_count).astype(f32)
    local = columns(local, HALF).astype(jnp.int32)
    lane = lax.broadcasted_iota(jnp.int32, (HALF, 128), 1)
    hot = (lane == local) | (lane == local + 16) | (lane == 15)
    sel[...] = jnp.where(hot, 1.0, 0.0).astype(bf16)


def usable_row(starts, first, count, row_count):
    time = lax.axis_index(axes) * row_count + first + lax.broadcasted_iota(jnp.int32, (1, count), 1)
    return jnp.where(time - DILATION >= starts[:, first : first + count], 1.0, 0.0)


def frame_terms(mel, prior, cond, bias, table, frames):
    slot_count = mel.shape[0]
    frames[...] = jnp.zeros((16, 128), f32)
    frames[slot_count : 2 * slot_count, :MELS] = mel[...]
    if prior is not None:
        frames[:slot_count, :MELS] = prior
    row = jnp.concatenate([bias[i : i + 1, :] for i in range(8)], 1)
    terms = exact(frames[:, :MELS], cond[...], NN) + row
    keep = lax.broadcasted_iota(jnp.int32, (16, GATE), 0) < 2 * slot_count
    high, low = split(jnp.where(keep, terms, 0.0))
    table[...] = jnp.zeros((128, GATE), bf16)
    table[0:16, :] = high
    table[16:32, :] = low


def gates(tanh_in, sigm_in, cols, gh, gl, ca, cb):
    th = jnp.tanh(tanh_in)
    sg = 0.5 * jnp.tanh(0.5 * sigm_in) + 0.5
    gated = th * sg
    gh[:, cols], gl[:, cols] = split(gated)
    ca[:, cols] = sg * (1.0 - th * th)
    cb[:, cols] = gated * (1.0 - sg)


def preact_block(dh, dl, sh, sl, sel, wh, wl, table, cols):
    left = jnp.concatenate(
        [dh[...], sh[...], dh[...], sh[...], dl[...], sl[...], sel[...]], 1
    )
    right = jnp.concatenate([wh[:, cols], wl[:, cols], wh[:, cols], table[:, cols]], 0)
    return dot(left, right, NN)


BLOCK = 256


def late_body(
    rows, signal, conv, cond_hbm, mel_hbm, slots_hbm, starts_hbm, bias_hbm,
    resid_hbm, skip_hbm, proj_hbm,
    held, sh0, sl0, sh1, sl1, dh, dl, wh, wl, sel, gh, gl, ca, cb,
    cond, mel, slots, starts, bias, resid_cotan, skip_cotan, proj,
    weights, table, frames, ssem, wsem, fsem, lsem,
):
    first = HALF - DILATION
    upper = pltpu.make_async_copy(
        signal.at[pl.ds(first, rows - first)], held.at[pl.ds(first, rows - first)], ssem.at[0]
    )
    lower = pltpu.make_async_copy(
        signal.at[pl.ds(0, first)], held.at[pl.ds(0, first)], ssem.at[1]
    )
    order = [c for j in range(HALF // BLOCK) for c in (j * BLOCK, HALF + j * BLOCK)]
    pieces = [
        pltpu.make_async_copy(
            conv.at[:, :, pl.ds(c, BLOCK)], weights.at[:, :, pl.ds(c, BLOCK)], wsem.at[i]
        )
        for i, c in enumerate(order)
    ]
    few = [
        pltpu.make_async_copy(a, b, fsem.at[i])
        for i, (a, b) in enumerate(
            ((slots_hbm, slots), (starts_hbm, starts), (mel_hbm, mel), (bias_hbm, bias), (cond_hbm, cond))
        )
    ]
    later = [
        pltpu.make_async_copy(a, b, lsem.at[i])
        for i, (a, b) in enumerate(
            ((resid_hbm, resid_cotan), (skip_hbm, skip_cotan), (proj_hbm, proj))
        )
    ]
    for copy in (*few, upper, *pieces, lower, *later):
        copy.start()
    for copy in few:
        copy.wait()
    picks(slots, 1, mel.shape[0], sel)
    frame_terms(mel, None, cond, bias, table, frames)
    usable = columns(usable_row(starts, HALF, HALF, rows), HALF)
    upper.wait()
    sh1[...], sl1[...] = split(held[HALF:, :])
    dh[...], dl[...] = split(held[first : first + HALF, :] * usable)
    for j in range(HALF // BLOCK):
        for i in (2 * j, 2 * j + 1):
            pieces[i].wait()
            cols = slice(order[i], order[i] + BLOCK)
            for tap in range(2):
                span = slice(tap * RESID, (tap + 1) * RESID)
                wh[span, cols], wl[span, cols] = split(weights[tap, :, cols])
        tc, sc = (slice(order[i], order[i] + BLOCK) for i in (2 * j, 2 * j + 1))
        tanh_in = preact_block(dh, dl, sh1, sl1, sel, wh, wl, table, tc)
        sigm_in = preact_block(dh, dl, sh1, sl1, sel, wh, wl, table, sc)
        gates(tanh_in, sigm_in, tc, gh, gl, ca, cb)
    lower.wait()
    sh0[0:first, :], sl0[0:first, :] = split(held[0:first, :])
    sh0[first:, :], sl0[first:, :] = split(held[first:HALF, :])
    for copy in later:
        copy.wait()


def early_body(
    rows, halo, sh, sl, wh, wl, cond, mel, slots, starts, bias, resid_cotan, skip_cotan, proj,
    dh, dl, sel, gh, gl, ca, cb, uh, ul, ph, plo, usum, table, frames,
):
    picks(slots, 0, mel.shape[0], sel)
    frame_terms(mel, halo[DILATION : DILATION + mel.shape[0], :MELS], cond, bias, table, frames)
    usable = columns(usable_row(starts, 0, HALF, rows), HALF)
    dh[0:DILATION, :], dl[0:DILATION, :] = split(halo[0:DILATION, :] * usable[0:DILATION])
    rest = HALF - DILATION
    for part, out in ((sh, dh), (sl, dl)):
        out[DILATION:, :] = (part[0:rest, :].astype(f32) * usable[DILATION:]).astype(bf16)
    for j in range(HALF // BLOCK):
        tc, sc = (slice(c + j * BLOCK, c + (j + 1) * BLOCK) for c in (0, HALF))
        tanh_in = preact_block(dh, dl, sh, sl, sel, wh, wl, table, tc)
        sigm_in = preact_block(dh, dl, sh, sl, sel, wh, wl, table, sc)
        gates(tanh_in, sigm_in, tc, gh, gl, ca, cb)
    for k, part in enumerate((resid_cotan, skip_cotan)):
        total = jnp.zeros((8, RESID), f32)
        span = slice(k * RESID, (k + 1) * RESID)
        for r in range(0, rows, 128):
            x = part[r : r + 128, :]
            uh[r : r + 128, span], ul[r : r + 128, span] = split(x)
            total = total + jnp.sum(x.reshape(16, 8, RESID), 0)
        usum[:, span] = total
    ph[...], plo[...] = split(proj[...])


def put_tiles(out, value, col0, stride=None):
    height, width = value.shape
    for r in range(height // 8):
        base = r * 8 if stride is None else (r * 8 // QUARTER) * stride + (r * 8) % QUARTER
        for c in range(width // 128):
            out[base + col0 // 128 + c] = value[8 * r : 8 * r + 8, 128 * c : 128 * c + 128]


WIDE = 512


def weight_grad(highs, lows, cols, rh, rl, out, stride=None):
    high = [h[:, cols] for h in highs]
    left = jnp.concatenate(high + high + [l[:, cols] for l in lows], 0)
    for c in range(0, GATE, WIDE):
        w = slice(c, c + WIDE)
        right = jnp.concatenate([rh[:, w], rl[:, w], rh[:, w]], 0)
        put_tiles(out, dot(left, right, TN), c, stride)


QUARTER = 128


def solve(pairs, args):
    (
        signal, item_start, frame_slot, mel_frames, resid_cotan, skip_cotan,
        conv_weight, cond_weight, proj_weight, biases,
        conv_moment, cond_moment, proj_moment, biases_moment,
        conv_average, cond_average, proj_average, biases_average,
    ) = args
    rows = signal.shape[0]
    slot_count = mel_frames.shape[0]
    slots = frame_slot.reshape(1, rows)
    starts = item_start.reshape(1, rows)
    bias = biases.reshape(16, 128)
    count = pairs.count
    order = Order()
    call = order.call

    def core_half(own):
        bit = pairs.bit(0)
        return bit if own else 1 - bit

    def half_cols(own):
        return pl.ds(pl.multiple_of(core_half(own) * 2 * QUARTER, 2 * QUARTER), 2 * QUARTER)

    (packed,) = call(
        lambda *r: pack_body(rows, *r), "pack", [signal, mel_frames],
        [((DILATION + 8, RESID), f32)], specs=[HBM, HBM],
        scratch=[pltpu.VMEM((slot_count, MELS), f32), pltpu.SemaphoreType.DMA((2,))],
    )
    halo = lax.ppermute(packed, axes, [(i, i + 1) for i in range(count - 1)])

    half = ((HALF, RESID), bf16)
    half32 = ((HALF, HALF), f32)
    square = ((GATE, GATE), bf16)
    pick = ((HALF, 128), bf16)
    small_scratch = [pltpu.VMEM((128, GATE), bf16), pltpu.VMEM((16, 128), f32)]
    held = [cond_weight, mel_frames, slots, starts, bias, resid_cotan, skip_cotan, proj_weight]
    (
        signal_in, sh0, sl0, sh1, sl1, dh1, dl1, wh, wl, sel1, gh1, gl1, ca1, cb1,
        cond_in, mel_in, slots, starts, bias_in, resid_in, skip_in, proj_in,
    ) = call(
        lambda *r: late_body(rows, *r), "late_gates", [signal, conv_weight, *held],
        [((rows, RESID), f32)] + [half] * 6 + [square] * 2 + [pick, half, half, half32, half32]
        + [(x.shape, x.dtype) for x in held],
        specs=[HBM] * 10,
        scratch=[pltpu.VMEM((2, RESID, GATE), f32), *small_scratch,
                 pltpu.SemaphoreType.DMA((2,)), pltpu.SemaphoreType.DMA((4,)),
                 pltpu.SemaphoreType.DMA((5,)), pltpu.SemaphoreType.DMA((3,))],
    )
    dh0, dl0, sel0, gh0, gl0, ca0, cb0, uh, ul, ph, plo, usum = call(
        lambda *r: early_body(rows, *r), "early_gates",
        [halo, sh0, sl0, wh, wl, cond_in, mel_in, slots, starts, bias_in, resid_in, skip_in, proj_in],
        [half, half, pick, half, half, half32, half32, square, square,
         ((HALF, GATE), bf16), ((HALF, GATE), bf16), ((8, GATE), f32)],
        scratch=small_scratch,
    )

    tiles = ((2 * QUARTER, 8, 128), f32)

    def proj_half(own):
        def body(gh0, gh1, gl0, gl1, uh, ul, out):
            weight_grad([gh0, gh1], [gl0, gl1], half_cols(own), uh, ul, out)

        return body

    gated = [gh0, gh1, gl0, gl1, uh, ul]
    (proj_send,) = call(proj_half(False), "proj_grad_send", gated, [tiles])
    proj_sum = Sum(order, pairs, "proj", proj_send, WHOLE[0])

    def gate_grad(gh0, gh1, gl0, gl1, uh, ul, ph, plo, ca0, ca1, cb0, cb1, out, gph, gpl):
        proj_half(True)(gh0, gh1, gl0, gl1, uh, ul, out)
        for r in range(0, rows, BLOCK):
            span = slice(r, r + BLOCK)
            left = jnp.concatenate([uh[span, :], uh[span, :], ul[span, :]], 1)
            right = jnp.concatenate([ph[...], plo[...], ph[...]], 1)
            grad = dot(left, right, NT)
            ca, cb = (ca0, cb0) if r < HALF else (ca1, cb1)
            inner = slice(r % HALF, r % HALF + BLOCK)
            gph[span, :HALF], gpl[span, :HALF] = split(grad * ca[inner, :])
            gph[span, HALF:], gpl[span, HALF:] = split(grad * cb[inner, :])

    proj_sum.rest, gph, gpl = call(
        gate_grad, "gate_grad", gated + [ph, plo, ca0, ca1, cb0, cb1], [tiles, square, square]
    )
    proj_sum.advance()

    def tap_half(own):
        def body(h0, h1, l0, l1, gph, gpl, out):
            weight_grad([h0, h1], [l0, l1], half_cols(own), gph, gpl, out)

        return body

    tap0 = [dh0, dh1, dl0, dl1, gph, gpl]
    (send,) = call(tap_half(False), "tap0_send", tap0, [tiles])
    tap0_sum = Sum(order, pairs, "tap0", send, WHOLE[1])

    few = 24
    while (QUARTER + few) % max(1, count // 4):
        few += 8
    quarter = QUARTER + few
    tap1 = [sh0, sh1, sl0, sl1, gph, gpl]
    wide_tiles = ((2 * quarter, 8, 128), f32)

    def tap1_half(own, sh0, sh1, sl0, sl1, gph, gpl, both, out):
        weight_grad([sh0, sh1], [sl0, sl1], half_cols(own), gph, gpl, out, quarter)
        for q in range(2):
            out[pl.ds(q * quarter + QUARTER, few)] = both[core_half(own) * 2 + q]

    def tap0_keep_tap1_send(
        dh0, dh1, dl0, dl1, gph, gpl, sh0, sh1, sl0, sl1, sel0, sel1, usum, mel, halo,
        zero_keep, one_send, both, frame_grad, frames,
    ):
        tap_half(True)(dh0, dh1, dl0, dl1, gph, gpl, zero_keep)
        sel = [sel0[:, 0:16], sel1[:, 0:16]]
        found = dot(
            jnp.concatenate(sel + sel, 0), jnp.concatenate([gph[...], gpl[...]], 0), TN
        )
        frame_grad[...] = found
        frames[...] = jnp.zeros((16, 128), f32)
        frames[:slot_count, :MELS] = halo[DILATION : DILATION + slot_count, :MELS]
        frames[slot_count : 2 * slot_count, :MELS] = mel[...]
        cond_grad = exact(frames[:, :MELS], found, TN)
        both[...] = jnp.zeros((4, few, 8, 128), f32)
        for q in range(4):
            part = cond_grad[24 * q : min(24 * q + 24, MELS), :]
            put_tiles(both.at[q], part, 0)
        sums = jnp.sum(usum[...], 0, keepdims=True)
        for i in range(8):
            lane = slice(128 * i, 128 * i + 128)
            both[3, 8, i : i + 1, :] = found[15:16, lane]
            both[3, 9, i : i + 1, :] = sums[:, lane]
        tap1_half(False, sh0, sh1, sl0, sl1, gph, gpl, both, one_send)

    tap0_sum.rest, send, few_grad, frame_grad = call(
        tap0_keep_tap1_send, "tap0_keep_tap1_send",
        tap0 + tap1[:4] + [sel0, sel1, usum, mel_in, halo],
        [tiles, wide_tiles, ((4, few, 8, 128), f32), ((16, GATE), f32)],
        scratch=[pltpu.VMEM((16, 128), f32)],
    )
    tap1_sum = Sum(order, pairs, "tap1", send, WHOLE[2])
    tap0_sum.advance()
    (tap1_sum.rest,) = call(
        lambda *r: tap1_half(True, *r), "tap1_keep", tap1 + [few_grad], [wide_tiles]
    )

    def back_body(gph, gpl, wh, wl, frame_grad, cond, starts, out, own):
        usable = columns(usable_row(starts, 0, 128, rows), 128)[0:DILATION]
        parts = [(p[0:DILATION, :].astype(f32) * usable).astype(bf16) for p in (gph, gpl)]
        left = jnp.concatenate([parts[0], parts[0], parts[1]], 1)
        right = jnp.concatenate([wh[0:RESID, :], wl[0:RESID, :], wh[0:RESID, :]], 1)
        out[0:DILATION, :] = dot(left, right, NT)
        mels = exact(frame_grad[...], cond[...], NT)
        out[DILATION:, :] = jnp.zeros((8, RESID), f32)
        out[DILATION : DILATION + slot_count, :MELS] = mels[:slot_count]
        own[...] = mels[slot_count : 2 * slot_count]

    state = {}

    def back():
        state["back"], state["mel_own"] = call(
            back_body, "back", [gph, gpl, wh, wl, frame_grad, cond_in, starts],
            [((DILATION + 8, RESID), f32), ((slot_count, MELS), f32)],
        )
        state["came"] = lax.ppermute(state["back"], axes, [(i, i - 1) for i in range(1, count)])

    def mix(r):
        def body(gh, gl, ph, plo, bias, signal, *refs):
            outs, (held, sem) = refs[-4:-2], refs[-2:]
            copies = []
            for s in range(0, HALF, BLOCK):
                inner = slice(s, s + BLOCK)
                span = slice(r + s, r + s + BLOCK)
                left = jnp.concatenate([gh[inner, :], gh[inner, :], gl[inner, :]], 1)
                for k, c in enumerate((0, RESID)):
                    w = slice(c, c + RESID)
                    right = jnp.concatenate([ph[:, w], plo[:, w], ph[:, w]], 0)
                    first = 8 + c // 128
                    row = jnp.concatenate([bias[i : i + 1, :] for i in range(first, first + 4)], 1)
                    mixed = dot(left, right, NN) + row
                    held[k, inner, :] = mixed + signal[span, :] if k == 0 else mixed
                    copies.append(
                        pltpu.make_async_copy(
                            held.at[k, pl.ds(s, BLOCK)],
                            outs[k].at[pl.ds(r + s, BLOCK)],
                            sem.at[len(copies)],
                        )
                    )
                    copies[-1].start()
            for copy in copies:
                copy.wait()

        gh, gl = (gh0, gl0) if r < HALF else (gh1, gl1)
        old = state.get("mixed", [])
        state["mixed"] = call(
            body, f"mix{r}", [gh, gl, ph, plo, bias_in, signal_in, *old],
            [((rows, RESID), f32)] * 2, aliases={6 + i: i for i in range(len(old))},
            specs=[VMEM] * 6 + [HBM] * len(old), out_specs=[HBM] * 2,
            scratch=[pltpu.VMEM((2, HALF, RESID), f32), pltpu.SemaphoreType.DMA((4,))],
        )

    def signal_grad(r):
        last = r + HALF == rows

        def body(gph, gpl, wh, wl, starts, resid_cotan, *refs):
            held, mels, sem = refs[-3:]
            copies = []
            if last:
                came, own, _, out, mel_grad = refs[:-3]
                mels[...] = own[...] + came[DILATION : DILATION + slot_count, :MELS]
                copies.append(pltpu.make_async_copy(mels, mel_grad, sem.at[2]))
                copies[0].start()
            else:
                out = refs[-4]
            usable = columns(usable_row(starts, 0, rows, rows), rows)
            right = jnp.concatenate(
                [w[s, :] for s in (slice(RESID, GATE), slice(0, RESID)) for w in (wh, wl, wh)], 1
            )
            for s in range(r, r + HALF, BLOCK):
                span = slice(s, s + BLOCK)
                ahead = slice(s + DILATION, min(s + DILATION + BLOCK, rows))
                later = []
                for p in (gph, gpl):
                    x = (p[ahead, :].astype(f32) * usable[ahead]).astype(bf16)
                    if s + BLOCK == rows:
                        x = jnp.concatenate([x, jnp.zeros((DILATION, GATE), bf16)], 0)
                    later.append(x)
                left = jnp.concatenate(
                    [gph[span, :], gph[span, :], gpl[span, :], later[0], later[0], later[1]], 1
                )
                inner = slice(s - r, s - r + BLOCK)
                held[inner, :] = dot(left, right, NT) + resid_cotan[span, :]
                if s + BLOCK == rows:
                    held[HALF - DILATION :, :] += came[0:DILATION, :]
                copies.append(
                    pltpu.make_async_copy(
                        held.at[pl.ds(s - r, BLOCK)], out.at[pl.ds(s, BLOCK)], sem.at[(s - r) // BLOCK]
                    )
                )
                copies[-1].start()
            for copy in copies:
                copy.wait()

        ins = [gph, gpl, wh, wl, starts, resid_in]
        outs = [((rows, RESID), f32)]
        if last:
            ins += [state["came"], state["mel_own"]]
            outs += [((slot_count, MELS), f32)]
        old = state.get("signal_grad", [])
        state["signal_grad"] = call(
            body, f"signal_grad{r}", ins + list(old), outs, aliases={len(ins): 0} if old else {},
            specs=[VMEM] * len(ins) + [HBM] * len(old), out_specs=[HBM] * len(outs),
            scratch=[pltpu.VMEM((HALF, RESID), f32), pltpu.VMEM((slot_count, MELS), f32),
                     pltpu.SemaphoreType.DMA((3,))],
        )

    root = math.sqrt(rows * count)
    conv_rate = step_scale / (math.sqrt(2 * RESID) * 1.5 * root)
    cond_rate = step_scale / (math.sqrt(MELS) * 1.5 * root)
    proj_rate = step_scale / (math.sqrt(GATE // 16) * 0.3 * root)
    biases_rate = step_scale * 0.3 / (1.2 * root)

    def step_tile(g, w, m, a, rate):
        m = momentum_rate * m + g
        w = w - rate * (g + momentum_rate * m)
        return w, m, ema_decay * a + (1.0 - ema_decay) * w

    def update(total, key, which, trio, lead, rate):
        shape = trio[0].shape
        old = state.get(key, [])
        pieces = [total.pieces[k] for k in which]

        def body(*refs):
            n = len(which)
            gs, trio_refs = refs[:n], refs[n : n + 3]
            outs = refs[n + 3 + len(old) : n + 7 + len(old)]
            held, sem = refs[n + 7 + len(old) : -1], refs[-1]
            ins = trio_refs if lead is None else [x.at[lead] for x in trio_refs]
            outs = outs if lead is None else [x.at[lead] for x in outs]
            copies = []
            for i, k in enumerate(which):
                sibling = k % 2 == 1
                core, bit = pairs.bit(0), pairs.bit(1, sibling)
                core = 1 - core if sibling else core
                bit = 1 - bit if k >= 2 else bit
                first = pl.multiple_of((core * 2 + bit) * QUARTER, QUARTER)
                for r in range(0, QUARTER, 16):
                    span = slice(i * QUARTER + r, i * QUARTER + r + 16)
                    there = pl.ds(first + r, 16)
                    for c in range(0, GATE, 128):
                        w = slice(c, c + 128)
                        tile = r + c // 128
                        g = jnp.concatenate([gs[i][tile], gs[i][tile + 8]], 0)
                        new = step_tile(g, *(x[there, w] for x in ins), rate)
                        for ref, value in zip(held, new):
                            ref[span, w] = value
                        held[3][span, w] = new[0].astype(bf16)
                for o in range(4):
                    copy = pltpu.make_async_copy(
                        held[o].at[pl.ds(i * QUARTER, QUARTER)],
                        outs[o].at[pl.ds(first, QUARTER)],
                        sem.at[i * 4 + o],
                    )
                    copy.start()
                    copies.append(copy)
            for copy in copies:
                copy.wait()

        n = len(which)
        kinds = (f32, f32, f32, bf16)
        state[key] = call(
            body, f"{total.name}_update{which[0]}", [*pieces, *trio, *old],
            [(shape, t) for t in kinds],
            specs=[VMEM] * (n + 3) + [HBM] * len(old), out_specs=[HBM] * 4,
            scratch=[pltpu.VMEM((n * QUARTER, GATE), t) for t in kinds]
            + [pltpu.SemaphoreType.DMA((4 * n,))],
            aliases={n + 3 + i: i for i in range(len(old))},
        )

    conv = (conv_weight, conv_moment, conv_average)
    matrices = {
        "proj": (proj_sum, "proj", (proj_weight, proj_moment, proj_average), None, proj_rate),
        "tap0": (tap0_sum, "conv", conv, 0, conv_rate),
        "tap1": (tap1_sum, "conv", conv, 1, conv_rate),
    }

    def spread(total):
        total.pieces = [total.piece, pairs.swap(total.piece, 0), pairs.swap(total.piece, 1)]

    def relay(total):
        total.pieces.append(pairs.swap(total.pieces[2], 0))

    def few_body(*refs):
        pieces = refs[:4]
        cw, cm, ca, bw, bm, ba = refs[4:10]
        grads, sem = refs[18], refs[-1]
        conds, biass = refs[19:23], refs[23:27]
        for k in range(4):
            sibling = k % 2 == 1
            core, bit = pairs.bit(0), pairs.bit(1, sibling)
            core = 1 - core if sibling else core
            bit = 1 - bit if k >= 2 else bit
            grads[pl.ds((core * 2 + bit) * 24, 24)] = pieces[k][QUARTER : QUARTER + 24]
        for r in range(0, MELS, 16):
            span = slice(r, r + 16)
            for c in range(0, GATE, 128):
                w = slice(c, c + 128)
                tile = r + c // 128
                g = jnp.concatenate([grads[tile], grads[tile + 8]], 0)
                new = step_tile(g, *(x[span, w] for x in (cw, cm, ca)), cond_rate)
                for ref, value in zip(conds, new):
                    ref[span, w] = value
                conds[3][span, w] = new[0].astype(bf16)
        grad = jnp.concatenate([grads[MELS], grads[MELS + 1]], 0)
        new = step_tile(grad, bw[...], bm[...], ba[...], biases_rate)
        for ref, value in zip(biass, new):
            ref[...] = value
        biass[3][...] = new[0].astype(bf16)
        copies = [
            pltpu.make_async_copy(a, b, sem.at[i])
            for i, (a, b) in enumerate(zip((*conds, *biass), refs[10:18]))
        ]
        for copy in copies:
            copy.start()
        for copy in copies:
            copy.wait()

    def few_update():
        kinds = (f32, f32, f32, bf16)
        state["few"] = call(
            few_body, "few_update",
            [*tap1_sum.pieces, cond_weight, cond_moment, cond_average,
             bias, biases_moment.reshape(16, 128), biases_average.reshape(16, 128)],
            [((MELS, GATE), t) for t in kinds] + [((16, 128), t) for t in kinds],
            out_specs=[HBM] * 8,
            scratch=[pltpu.VMEM((96, 8, 128), f32)]
            + [pltpu.VMEM((MELS, GATE), t) for t in kinds] + [pltpu.VMEM((16, 128), t) for t in kinds]
            + [pltpu.SemaphoreType.DMA((8,))],
        )

    trees = {"P": proj_sum, "0": tap0_sum, "1": tap1_sum}
    names = {"P": "proj", "0": "tap0", "1": "tap1"}
    acts = {"back": back, "few": few_update}
    for i in range(2):
        acts[f"mix{i}"] = lambda i=i: mix(i * HALF)
        acts[f"sg{i}"] = lambda i=i: signal_grad(i * HALF)
    for k, t in trees.items():
        first, second, low, high = (
            (lambda w=w, k=k: update(*matrices[names[k]][:2], w, *matrices[names[k]][2:]))
            for w in ((0, 1), (2, 3), (2,), (3,))
        )
        acts.update({f"s{k}": lambda t=t: spread(t), f"r{k}": lambda t=t: relay(t)})
        acts.update({f"u{k}": first, f"v{k}": second, f"w{k}": low, f"x{k}": high})
    for word in SCRIPT.split():
        if word in trees:
            trees[word].advance()
        elif word[0] == "s" and word[1:] in trees:
            while not trees[word[1:]].done:
                trees[word[1:]].advance()
            acts[word]()
        else:
            acts[word]()
    proj_new, conv_new = state["proj"], state["conv"]
    cond_new, bias_new = state["few"][:4], [x.reshape(-1) for x in state["few"][4:]]
    result = [*state["mixed"], *state["signal_grad"]]
    for k in range(4):
        result += [conv_new[k], cond_new[k], proj_new[k], bias_new[k]]
    return tuple(result)


WHOLE = (2, 1, 1)
SCRIPT = """
mix0 P 1 0 back P 1 0 mix1 P 0 1 sg0 P 0 1 P sP 0 1 sg1 rP uP 0 s0 1 s1 vP u0 r0 u1 r1 w0 w1 few x0 x1
"""


def shards(*args):
    return solve(Pairs(), args)


def solution(mesh):
    rows = P(("blk", "seq"), None)
    in_specs = (rows, P(("blk", "seq")), P(("blk", "seq")), rows, rows, rows) + (P(),) * 12
    out_specs = (rows,) * 4 + (P(),) * 16
    return jax.shard_map(shards, mesh=mesh, in_specs=in_specs, out_specs=out_specs, check_vma=False)
```

```python
import math

import jax
import jax.numpy as jnp
from jax import lax
from jax.experimental import pallas as pl
from jax.experimental.pallas import tpu as pltpu
from jax.sharding import PartitionSpec as P

RESID = 512
GATE = 1024
MELS = 80
DILATION = 64
HALF = 512

f32 = jnp.float32
bf16 = jnp.bfloat16
momentum_rate = 0.9
ema_decay = 0.5
step_scale = 0.15
axes = ("blk", "seq")

VMEM = pl.BlockSpec(memory_space=pltpu.VMEM)
HBM = pl.BlockSpec(memory_space=pltpu.HBM)
ANY = pl.BlockSpec(memory_space=pl.ANY)
MIB = 1 << 20


TOKEN = ((8, 128), f32)

RATE = 3.2e9
TIMES = {
    "pack": 1, "late_gates": 8, "early_gates": 6, "proj_grad_send": 1.8, "gate_grad": 5.8,
    "tap0_send": 1.8, "tap0_keep_tap1_send": 4.5, "tap1_keep": 1.8, "mix": 2.8, "signal_grad": 4.4,
    "back": 1.4, "update1_few": 2, "update1": 1.4, "update2": 2, "update3": 2.7, "update4": 3.3,
}
FOLD = 0.1


def expected(name):
    for key in sorted(TIMES, key=len, reverse=True):
        if key in name:
            return TIMES[key]
    return FOLD


class Order:
    def __init__(self):
        self.last = None

    def call(
        self, body, name, ins, outs, specs=None, out_specs=None, scratch=(), limit=16, aliases=None
    ):
        specs = list(specs) if specs else [VMEM] * len(ins)
        ins = [
            pltpu.with_memory_space_constraint(x, pltpu.HBM) if s is HBM else x
            for x, s in zip(ins, specs)
        ]
        out_specs = list(out_specs) if out_specs else [VMEM] * len(outs)
        after = [] if self.last is None else [self.last]
        n_in, n_after, n_out = len(ins), len(after), len(outs)

        def run(*refs):
            outs = refs[n_in + n_after : n_in + n_after + n_out]
            token = refs[n_in + n_after + n_out]
            token[...] = jnp.zeros(token.shape, f32)
            body(*refs[:n_in], *outs, *refs[n_in + n_after + n_out + 1 :])

        kinds = {id(VMEM): pltpu.VMEM, id(HBM): pltpu.HBM}
        *result, self.last = pl.pallas_call(
            run,
            out_shape=[kinds[id(s)](*o) for o, s in zip(outs, out_specs)] + [pltpu.VMEM(*TOKEN)],
            in_specs=specs + [VMEM] * n_after,
            out_specs=out_specs + [VMEM],
            scratch_shapes=list(scratch),
            input_output_aliases=aliases or {},
            compiler_params=pltpu.CompilerParams(vmem_limit_bytes=limit * MIB),
            cost_estimate=pl.CostEstimate(
                flops=int(RATE * expected(name)), bytes_accessed=1, transcendentals=0
            ),
            name=name,
        )(*ins, *after)
        return result


wide8 = jnp.float8_e5m2
fine8 = jnp.float8_e4m3fn
SIGNAL_SCALE, CONV_SCALE, GRAD_SCALE = 2.0**12, 2.0**18, 2.0**3
UP_SCALE, PROJ_SCALE, GATED_SCALE = 2.0**6, 2.0**9, 2.0**8
LOW = 256.0


def split(x):
    high = x.astype(bf16)
    return high, (x - high.astype(f32)).astype(bf16)


def put(refs, where, x, scale):
    high = x.astype(bf16)
    refs[0][where] = high
    refs[1][where] = (high * bf16(scale)).astype(refs[1].dtype)
    refs[2][where] = ((x - high.astype(f32)) * (scale * LOW)).astype(refs[2].dtype)


def dot(left, right, over):
    return lax.dot_general(left, right, (over, ((), ())), preferred_element_type=f32)


def product(left, right, over, scale):
    axis = [o[0] for o in over]
    low = jnp.concatenate([left[2], left[1]], axis[0])
    high = jnp.concatenate([right[1], right[2]], axis[1])
    return dot(left[0], right[0], over) + dot(low, high, over) * (1.0 / (LOW * scale))


def exact(left, right, over):
    return lax.dot_general(
        left, right, (over, ((), ())), preferred_element_type=f32, precision=lax.Precision.HIGHEST
    )


NN = ((1,), (0,))
NT = ((1,), (1,))
TN = ((0,), (0,))


ORDERS = {
    "proj": ((2, 1, 3, 4), (1, 2, 4, 3)),
    "tap0": ((2, 3, 1, 4), (1, 4, 2, 3)),
    "tap1": ((2, 1, 3, 4), (1, 2, 4, 3)),
}
LARGE = ((6, 0, 3, 7, 1, 4, 5), (0, 6, 3, 1, 7, 4, 5))


def plan(blk, seq, name):
    if (blk, seq) == (8, 4):
        return 0, ORDERS[name]
    if (blk, seq) == (64, 4):
        return 2, LARGE
    rest = tuple(range(1, (blk * seq).bit_length() - 1))
    return 0, (rest, rest)


class Pairs:
    def __init__(self, name):
        blk, seq = lax.axis_size("blk"), lax.axis_size("seq")
        self.count = blk * seq
        self.core_bit, (first, second) = plan(blk, seq, name)
        self.places = [(self.core_bit, self.core_bit), *zip(first, second)]
        self.steps = len(self.places)
        self.pairs = [
            [(i, i ^ (1 << p[(i >> self.core_bit) & 1])) for i in range(self.count)]
            for p in self.places
        ]

    def bit(self, step, sibling=False):
        me = lax.axis_index(axes)
        core = (me >> self.core_bit) & 1
        if sibling:
            core = 1 - core
        if step == 0:
            return core
        a, b = self.places[step]
        return jnp.where(core == 0, (me >> a) & 1, (me >> b) & 1)

    def quarter(self, k):
        core, bit = self.bit(0), self.bit(1, k % 2 == 1)
        return (1 - core if k % 2 else core) * 2 + (1 - bit if k >= 2 else bit)

    def swap(self, x, step):
        return lax.ppermute(x, axes, self.pairs[step])


class Sum:
    def __init__(self, order, pairs, name, send, whole=1):
        self.order, self.pairs, self.name = order, pairs, name
        self.parted = pairs.steps - whole
        self.step, self.back = 0, False
        self.got = pairs.swap(send, 0)
        self.done = False

    def advance(self):
        if self.done:
            return
        pairs, step = self.pairs, self.step
        label = f"{self.name}_{'join' if self.back else 'fold'}{step}"
        if self.back:
            size = self.piece.shape[0]

            def body(mine, got, out):
                bit = pairs.bit(step)
                out[pl.ds(bit * size, size)] = mine[...]
                out[pl.ds((1 - bit) * size, size)] = got[...]

            (self.piece,) = self.order.call(
                body, label, [self.piece, self.got], [((2 * size, 8, 128), f32)]
            )
            self.step -= 1
        elif step + 1 < self.parted:
            half = self.rest.shape[0] // 2

            def body(keep, got, send, rest):
                bit = pairs.bit(step + 1)
                here, there = pl.ds(bit * half, half), pl.ds((1 - bit) * half, half)
                send[...] = keep[there] + got[there]
                rest[...] = keep[here] + got[here]

            shape = ((half, 8, 128), f32)
            send, self.rest = self.order.call(body, label, [self.rest, self.got], [shape, shape])
            self.step += 1
            self.got = pairs.swap(send, self.step)
            return
        else:
            mine = self.rest if step < self.parted else self.piece

            def body(mine, got, out):
                out[...] = mine[...] + got[...]

            (self.piece,) = self.order.call(body, label, [mine, self.got], [(mine.shape, f32)])
            self.step += 1
            if self.step == pairs.steps:
                self.back, self.step = True, self.parted - 1
        if self.back and self.step == 1:
            self.done = True
            return
        self.got = pairs.swap(self.piece, self.step)


def pack_body(rows, signal, mel, out, frames, sem):
    copy = pltpu.make_async_copy(
        signal.at[pl.ds(rows - DILATION, DILATION)], out.at[pl.ds(0, DILATION)], sem.at[0]
    )
    other = pltpu.make_async_copy(mel, frames, sem.at[1])
    copy.start()
    other.start()
    out[DILATION:, :] = jnp.zeros((8, RESID), f32)
    other.wait()
    out[DILATION : DILATION + mel.shape[0], :MELS] = frames[...]
    copy.wait()


def columns(row, rows):
    return jnp.transpose(jnp.broadcast_to(row, (8, rows)))[:, :1]


def picks(slots, part, slot_count, sel):
    me = lax.axis_index(axes)
    local = (slots[:, part * HALF : (part + 1) * HALF] - (me - 1) * slot_count).astype(f32)
    local = columns(local, HALF).astype(jnp.int32)
    lane = lax.broadcasted_iota(jnp.int32, (HALF, 128), 1)
    hot = (lane == local) | (lane == local + 16) | (lane == 15)
    sel[...] = jnp.where(hot, 1.0, 0.0).astype(bf16)


def usable_row(starts, first, count, row_count):
    time = lax.axis_index(axes) * row_count + first + lax.broadcasted_iota(jnp.int32, (1, count), 1)
    return jnp.where(time - DILATION >= starts[:, first : first + count], 1.0, 0.0)


def frame_terms(mel, prior, cond, bias, table, frames):
    slot_count = mel.shape[0]
    frames[...] = jnp.zeros((16, 128), f32)
    frames[slot_count : 2 * slot_count, :MELS] = mel[...]
    if prior is not None:
        frames[:slot_count, :MELS] = prior
    row = jnp.concatenate([bias[i : i + 1, :] for i in range(8)], 1)
    terms = exact(frames[:, :MELS], cond[...], NN) + row
    keep = lax.broadcasted_iota(jnp.int32, (16, GATE), 0) < 2 * slot_count
    high, low = split(jnp.where(keep, terms, 0.0))
    table[...] = jnp.zeros((128, GATE), bf16)
    table[0:16, :] = high
    table[16:32, :] = low


def gates(tanh_in, sigm_in, cols, g, ca, cb):
    th = jnp.tanh(tanh_in)
    sg = 0.5 * jnp.tanh(0.5 * sigm_in) + 0.5
    gated = th * sg
    put(g, (slice(None), cols), gated, GATED_SCALE)
    ca[:, cols] = sg * (1.0 - th * th)
    cb[:, cols] = gated * (1.0 - sg)


def preact_block(d, x, sel, w, table, cols):
    main = dot(
        jnp.concatenate([d[0][...], x[0][...], sel[...]], 1),
        jnp.concatenate([w[0][:, cols], table[:, cols]], 0),
        NN,
    )
    low = dot(
        jnp.concatenate([d[2][...], x[2][...], d[1][...], x[1][...]], 1),
        jnp.concatenate([w[1][:, cols], w[2][:, cols]], 0),
        NN,
    )
    return main + low * (1.0 / (LOW * SIGNAL_SCALE * CONV_SCALE))


BLOCK = 256


def late_body(rows, *refs):
    signal, conv, cond, mel, slots, starts, bias = refs[:7]
    far, near, (table, frames, sem) = refs[7:10], refs[28:31], refs[31:]
    x0, x1, d, w = (refs[i : i + 3] for i in (10, 13, 16, 19))
    sel, g, ca, cb = refs[22], refs[23:26], refs[26], refs[27]
    copies = [pltpu.make_async_copy(a, b, sem.at[i]) for i, (a, b) in enumerate(zip(far, near))]
    for copy in copies:
        copy.start()
    first = HALF - DILATION
    picks(slots, 1, mel.shape[0], sel)
    frame_terms(mel, None, cond, bias, table, frames)
    usable = columns(usable_row(starts, HALF, HALF, rows), HALF)
    put(x1, slice(None), signal[HALF:, :], SIGNAL_SCALE)
    put(d, slice(None), signal[first : first + HALF, :] * usable, SIGNAL_SCALE)
    for j in range(HALF // BLOCK):
        blocks = [slice(c + j * BLOCK, c + (j + 1) * BLOCK) for c in (0, HALF)]
        products = []
        for cols in blocks:
            for tap in range(2):
                span = slice(tap * RESID, (tap + 1) * RESID)
                put(w, (span, cols), conv[tap, :, cols], CONV_SCALE)
            products.append(preact_block(d, x1, sel, w, table, cols))
        gates(*products, blocks[0], g, ca, cb)
    put(x0, slice(None), signal[0:HALF, :], SIGNAL_SCALE)
    for copy in copies:
        copy.wait()


def early_body(rows, *refs):
    halo, signal = refs[:2]
    x, w = refs[2:5], refs[5:8]
    cond, mel, slots, starts, bias, resid_cotan, skip_cotan, proj = refs[8:16]
    d, sel, g, ca, cb = refs[16:19], refs[19], refs[20:23], refs[23], refs[24]
    u, p, usum, table, frames = refs[25:28], refs[28:31], *refs[31:]
    picks(slots, 0, mel.shape[0], sel)
    frame_terms(mel, halo[DILATION : DILATION + mel.shape[0], :MELS], cond, bias, table, frames)
    usable = columns(usable_row(starts, 0, HALF, rows), HALF)
    put(d, slice(0, DILATION), halo[0:DILATION, :] * usable[0:DILATION], SIGNAL_SCALE)
    rest = HALF - DILATION
    put(d, slice(DILATION, None), signal[0:rest, :] * usable[DILATION:], SIGNAL_SCALE)
    usum[...] = jnp.zeros((8, 2 * RESID), f32)

    def part_cotangents(first, count):
        for r in range(first, first + count, 128):
            for k, part in enumerate((resid_cotan, skip_cotan)):
                span = slice(k * RESID, (k + 1) * RESID)
                value = part[r : r + 128, :]
                put(u, (slice(r, r + 128), span), value, UP_SCALE)
                usum[:, span] += jnp.sum(value.reshape(16, 8, RESID), 0)

    for j in range(HALF // BLOCK):
        tc, sc = (slice(c + j * BLOCK, c + (j + 1) * BLOCK) for c in (0, HALF))
        tanh_in = preact_block(d, x, sel, w, table, tc)
        part_cotangents(j * rows // 2, rows // 4)
        sigm_in = preact_block(d, x, sel, w, table, sc)
        part_cotangents(j * rows // 2 + rows // 4, rows // 4)
        gates(tanh_in, sigm_in, tc, g, ca, cb)
    put(p, slice(None), proj[...], PROJ_SCALE)


def put_tiles(out, value, col0, stride=None):
    height, width = value.shape
    for r in range(height // 8):
        base = r * 8 if stride is None else (r * 8 // QUARTER) * stride + (r * 8) % QUARTER
        for c in range(width // 128):
            out[base + col0 // 128 + c] = value[8 * r : 8 * r + 8, 128 * c : 128 * c + 128]


WIDE = 512


def weight_grad(left, cols, right, out, scale, stride=None):
    left = [jnp.concatenate([a[:, cols], b[:, cols]], 0) for a, b in zip(left[:3], left[3:])]
    for c in range(0, GATE, WIDE):
        wide = [r[:, c : c + WIDE] for r in right]
        put_tiles(out, product(left, wide, TN, scale), c, stride)


QUARTER = 128


def solve(pairs, args):
    (
        signal, item_start, frame_slot, mel_frames, resid_cotan, skip_cotan,
        conv_weight, cond_weight, proj_weight, biases,
        conv_moment, cond_moment, proj_moment, biases_moment,
        conv_average, cond_average, proj_average, biases_average,
    ) = args
    rows = signal.shape[0]
    slot_count = mel_frames.shape[0]
    slots = frame_slot.reshape(1, rows)
    starts = item_start.reshape(1, rows)
    bias = biases.reshape(16, 128)
    count = pairs.count
    order = Order()
    call = order.call

    def core_half(own):
        bit = pairs.bit(0)
        return bit if own else 1 - bit

    def half_cols(own):
        return pl.ds(pl.multiple_of(core_half(own) * 2 * QUARTER, 2 * QUARTER), 2 * QUARTER)

    (packed,) = call(
        lambda *r: pack_body(rows, *r), "pack", [signal, mel_frames],
        [((DILATION + 8, RESID), f32)], specs=[HBM, HBM],
        scratch=[pltpu.VMEM((slot_count, MELS), f32), pltpu.SemaphoreType.DMA((2,))],
    )
    halo = lax.ppermute(packed, axes, [(i, i + 1) for i in range(count - 1)])

    wide, fine = (bf16, wide8, wide8), (bf16, fine8, fine8)
    half = [((HALF, RESID), t) for t in wide]
    half_gate = [((HALF, RESID), t) for t in fine]
    half32 = ((HALF, HALF), f32)
    square = [((GATE, GATE), t) for t in wide]
    pick = ((HALF, 128), bf16)
    small_scratch = [pltpu.VMEM((128, GATE), bf16), pltpu.VMEM((16, 128), f32)]
    held = [resid_cotan, skip_cotan, proj_weight]
    out = call(
        lambda *r: late_body(rows, *r), "late_gates",
        [signal, conv_weight, cond_weight, mel_frames, slots, starts, bias, *held],
        [*half, *half, *half, *square, pick, *half_gate, half32, half32, *((x.shape, x.dtype) for x in held)],
        specs=[VMEM] * 7 + [HBM] * 3,
        scratch=[*small_scratch, pltpu.SemaphoreType.DMA((3,))],
    )
    x0, x1, d1, w = (out[i : i + 3] for i in (0, 3, 6, 9))
    sel1, g1, ca1, cb1, (resid_in, skip_in, proj_in) = out[12], out[13:16], out[16], out[17], out[18:]
    out = call(
        lambda *r: early_body(rows, *r), "early_gates",
        [halo, signal, *x0, *w, cond_weight, mel_frames, slots, starts, bias, resid_in, skip_in, proj_in],
        [*half, pick, *half_gate, half32, half32, *(((GATE, GATE), t) for t in fine),
         *(((HALF, GATE), t) for t in fine), ((8, GATE), f32)],
        scratch=small_scratch,
    )
    d0, sel0, g0, ca0, cb0 = out[0:3], out[3], out[4:7], out[7], out[8]
    u, p, usum = out[9:12], out[12:15], out[15]

    tiles = ((2 * QUARTER, 8, 128), f32)

    def proj_half(own):
        def body(*refs):
            weight_grad(refs[:6], half_cols(own), refs[6:9], refs[9], GATED_SCALE * UP_SCALE)

        return body

    gated = [*g0, *g1, *u]
    (proj_send,) = call(proj_half(False), "proj_grad_send", gated, [tiles])
    proj_sum = Sum(order, pairs, "proj", proj_send, WHOLE[0])

    def gate_grad(*refs):
        u, p, (ca0, ca1, cb0, cb1) = refs[6:9], refs[9:12], refs[12:16]
        out, gp = refs[16], refs[17:20]
        proj_half(True)(*refs[:9], out)
        right = [x[...] for x in p]
        for r in range(0, rows, BLOCK):
            span = slice(r, r + BLOCK)
            grad = product([x[span, :] for x in u], right, NT, UP_SCALE * PROJ_SCALE)
            ca, cb = (ca0, cb0) if r < HALF else (ca1, cb1)
            inner = slice(r % HALF, r % HALF + BLOCK)
            put(gp, (span, slice(0, HALF)), grad * ca[inner, :], GRAD_SCALE)
            put(gp, (span, slice(HALF, GATE)), grad * cb[inner, :], GRAD_SCALE)

    proj_sum.rest, *gp = call(
        gate_grad, "gate_grad", [*gated, *p, ca0, ca1, cb0, cb1], [tiles, *square]
    )
    proj_sum.advance()

    def tap_half(own, stride=None):
        def body(*refs):
            weight_grad(
                refs[:6], half_cols(own), refs[6:9], refs[9], SIGNAL_SCALE * GRAD_SCALE, stride
            )

        return body

    (send,) = call(tap_half(False), "tap0_send", [*d0, *d1, *gp], [tiles])
    tap0_sum = Sum(order, Pairs("tap0"), "tap0", send, WHOLE[1])

    few = 24
    while (QUARTER + few) % max(1, count // 4):
        few += 8
    quarter = QUARTER + few
    wide_tiles = ((2 * quarter, 8, 128), f32)

    def tap1_half(own, *refs):
        both, out = refs[9:]
        tap_half(own, quarter)(*refs[:9], out)
        for q in range(2):
            out[pl.ds(q * quarter + QUARTER, few)] = both[core_half(own) * 2 + q]

    def tap0_keep_tap1_send(*refs):
        d, x, gp, (sel0, sel1, usum, mel, halo) = refs[:6], refs[6:12], refs[12:15], refs[15:20]
        zero_keep, one_send, both, frame_grad, frames = refs[20:]
        tap_half(True)(*d, *gp, zero_keep)
        sel = jnp.concatenate([sel0[:, 0:16], sel1[:, 0:16]], 0)
        found = dot(sel, gp[0][...], TN)
        found += dot(sel.astype(wide8), gp[2][...], TN) * (1.0 / (LOW * GRAD_SCALE))
        frame_grad[...] = found
        frames[...] = jnp.zeros((16, 128), f32)
        frames[:slot_count, :MELS] = halo[DILATION : DILATION + slot_count, :MELS]
        frames[slot_count : 2 * slot_count, :MELS] = mel[...]
        cond_grad = exact(frames[:, :MELS], found, TN)
        both[...] = jnp.zeros((4, few, 8, 128), f32)
        for q in range(4):
            part = cond_grad[24 * q : min(24 * q + 24, MELS), :]
            put_tiles(both.at[q], part, 0)
        sums = jnp.sum(usum[...], 0, keepdims=True)
        for i in range(8):
            lane = slice(128 * i, 128 * i + 128)
            both[3, 8, i : i + 1, :] = found[15:16, lane]
            both[3, 9, i : i + 1, :] = sums[:, lane]
        tap1_half(False, *x, *gp, both, one_send)

    tap0_sum.rest, send, few_grad, frame_grad = call(
        tap0_keep_tap1_send, "tap0_keep_tap1_send",
        [*d0, *d1, *x0, *x1, *gp, sel0, sel1, usum, mel_frames, halo],
        [tiles, wide_tiles, ((4, few, 8, 128), f32), ((16, GATE), f32)],
        scratch=[pltpu.VMEM((16, 128), f32)],
    )
    tap1_sum = Sum(order, Pairs("tap1"), "tap1", send, WHOLE[2])
    tap0_sum.advance()
    (tap1_sum.rest,) = call(
        lambda *r: tap1_half(True, *r), "tap1_keep", [*x0, *x1, *gp, few_grad], [wide_tiles]
    )

    def tap_back(gp, w, rows_, tap):
        span = slice(tap * RESID, (tap + 1) * RESID)
        return product(
            [x[rows_, :] for x in gp], [x[span, :] for x in w], NT, GRAD_SCALE * CONV_SCALE
        )

    def back_body(*refs):
        gp, w, (frame_grad, cond, starts, out, own) = refs[:3], refs[3:6], refs[6:]
        usable = columns(usable_row(starts, 0, 128, rows), 128)[0:DILATION]
        out[0:DILATION, :] = tap_back(gp, w, slice(0, DILATION), 0) * usable
        mels = exact(frame_grad[...], cond[...], NT)
        out[DILATION:, :] = jnp.zeros((8, RESID), f32)
        out[DILATION : DILATION + slot_count, :MELS] = mels[:slot_count]
        own[...] = mels[slot_count : 2 * slot_count]

    state = {}

    def back():
        state["back"], state["mel_own"] = call(
            back_body, "back", [*gp, *w, frame_grad, cond_weight, starts],
            [((DILATION + 8, RESID), f32), ((slot_count, MELS), f32)],
        )
        state["came"] = lax.ppermute(state["back"], axes, [(i, i - 1) for i in range(1, count)])

    def mix(r):
        def body(*refs):
            g, p, (bias, signal) = refs[:3], refs[3:6], refs[6:8]
            outs, (held, sem) = refs[-4:-2], refs[-2:]
            copies = []
            for s in range(0, HALF, BLOCK):
                inner = slice(s, s + BLOCK)
                span = slice(r + s, r + s + BLOCK)
                left = [x[inner, :] for x in g]
                for k, c in enumerate((0, RESID)):
                    w = slice(c, c + RESID)
                    first = 8 + c // 128
                    row = jnp.concatenate([bias[i : i + 1, :] for i in range(first, first + 4)], 1)
                    mixed = product(left, [x[:, w] for x in p], NN, GATED_SCALE * PROJ_SCALE) + row
                    held[k, inner, :] = mixed + signal[span, :] if k == 0 else mixed
                    copies.append(
                        pltpu.make_async_copy(
                            held.at[k, pl.ds(s, BLOCK)],
                            outs[k].at[pl.ds(r + s, BLOCK)],
                            sem.at[len(copies)],
                        )
                    )
                    copies[-1].start()
            for copy in copies:
                copy.wait()

        old = state.get("mixed", [])
        state["mixed"] = call(
            body, f"mix{r}", [*(g0 if r < HALF else g1), *p, bias, signal, *old],
            [((rows, RESID), f32)] * 2, aliases={8 + i: i for i in range(len(old))},
            specs=[VMEM] * 8 + [HBM] * len(old), out_specs=[HBM] * 2,
            scratch=[pltpu.VMEM((2, HALF, RESID), f32), pltpu.SemaphoreType.DMA((4,))],
        )

    def signal_grad(r):
        last = r + HALF == rows

        def body(*refs):
            gp, w, (starts, resid_cotan) = refs[:3], refs[3:6], refs[6:8]
            held, mels, sem = refs[-3:]
            copies = []
            if last:
                came, own, _, out, mel_grad = refs[8:-3]
                mels[...] = own[...] + came[DILATION : DILATION + slot_count, :MELS]
                copies.append(pltpu.make_async_copy(mels, mel_grad, sem.at[2]))
                copies[0].start()
            else:
                out = refs[-4]
            usable = columns(usable_row(starts, 0, rows, rows), rows)
            for s in range(r, r + HALF, BLOCK):
                span = slice(s, s + BLOCK)
                ahead = slice(s + DILATION, min(s + DILATION + BLOCK, rows))
                inner = slice(s - r, s - r + BLOCK)
                later = tap_back(gp, w, ahead, 0) * usable[ahead]
                held[inner, :] = tap_back(gp, w, span, 1) + resid_cotan[span, :]
                held[s - r : s - r + later.shape[0], :] += later
                if s + BLOCK == rows:
                    held[HALF - DILATION :, :] += came[0:DILATION, :]
                copies.append(
                    pltpu.make_async_copy(
                        held.at[pl.ds(s - r, BLOCK)], out.at[pl.ds(s, BLOCK)], sem.at[(s - r) // BLOCK]
                    )
                )
                copies[-1].start()
            for copy in copies:
                copy.wait()

        ins = [*gp, *w, starts, resid_in]
        outs = [((rows, RESID), f32)]
        if last:
            ins += [state["came"], state["mel_own"]]
            outs += [((slot_count, MELS), f32)]
        old = state.get("signal_grad", [])
        state["signal_grad"] = call(
            body, f"signal_grad{r}", ins + list(old), outs, aliases={len(ins): 0} if old else {},
            specs=[VMEM] * len(ins) + [HBM] * len(old), out_specs=[HBM] * len(outs),
            scratch=[pltpu.VMEM((HALF, RESID), f32), pltpu.VMEM((slot_count, MELS), f32),
                     pltpu.SemaphoreType.DMA((3,))],
        )

    root = math.sqrt(rows * count)
    conv_rate = step_scale / (math.sqrt(2 * RESID) * 1.5 * root)
    cond_rate = step_scale / (math.sqrt(MELS) * 1.5 * root)
    proj_rate = step_scale / (math.sqrt(GATE // 16) * 0.3 * root)
    biases_rate = step_scale * 0.3 / (1.2 * root)

    def step_tile(g, w, m, a, rate):
        m = momentum_rate * m + g
        w = w - rate * (g + momentum_rate * m)
        return w, m, ema_decay * a + (1.0 - ema_decay) * w

    conv = (conv_weight, conv_moment, conv_average)
    matrices = {
        "proj": ((proj_weight, proj_moment, proj_average), proj_rate),
        "conv": (conv, conv_rate),
    }
    kinds = (f32, f32, f32, bf16)
    few_args = (cond_weight, cond_moment, cond_average, bias,
                biases_moment.reshape(16, 128), biases_average.reshape(16, 128))
    few_shapes = [((MELS, GATE), t) for t in kinds] + [((16, 128), t) for t in kinds]

    def update_few(pieces, ins, outs, held, grads, sem):
        for k, piece in enumerate(pieces):
            first = tap1_sum.pairs.quarter(k) * 24
            grads[pl.ds(first, 24)] = piece[QUARTER : QUARTER + 24]
        for r in range(0, MELS, 16):
            span = slice(r, r + 16)
            for c in range(0, GATE, 128):
                w = slice(c, c + 128)
                tile = r + c // 128
                g = jnp.concatenate([grads[tile], grads[tile + 8]], 0)
                new = step_tile(g, *(x[span, w] for x in ins[:3]), cond_rate)
                for ref, value in zip(held, new):
                    ref[span, w] = value
                held[3][span, w] = new[0].astype(bf16)
        grad = jnp.concatenate([grads[MELS], grads[MELS + 1]], 0)
        new = step_tile(grad, *(x[...] for x in ins[3:]), biases_rate)
        for ref, value in zip(held[4:], new):
            ref[...] = value
        held[7][...] = new[0].astype(bf16)
        copies = [
            pltpu.make_async_copy(a, b, sem.at[i]) for i, (a, b) in enumerate(zip(held, outs))
        ]
        for copy in copies:
            copy.start()
        return copies

    def update(key, items, few_too=False):
        trio, rate = matrices[key]
        old = state.get(key, [])
        n = len(items)
        ins = [total.pieces[k] for total, k, _ in items] + [*trio]
        if few_too:
            ins += [*tap1_sum.pieces, *few_args]

        def body(*refs):
            refs = list(refs)
            take = lambda count: [refs.pop(0) for _ in range(count)]
            gs, trio_refs = take(n), take(3)
            few_refs = take(10) if few_too else []
            take(len(old))
            outs = take(4)
            few_outs = take(8) if few_too else []
            held, sem = take(4), refs.pop(0)
            copies = []
            if few_too:
                copies += update_few(
                    few_refs[:4], few_refs[4:], few_outs, refs[:8], refs[8], refs[9]
                )
            for i, (total, k, lead) in enumerate(items):
                first = pl.multiple_of(total.pairs.quarter(k) * QUARTER, QUARTER)
                parts = [x if lead is None else x.at[lead] for x in (*trio_refs, *outs)]
                for r in range(0, QUARTER, 16):
                    span = slice(i * QUARTER + r, i * QUARTER + r + 16)
                    there = pl.ds(first + r, 16)
                    for c in range(0, GATE, 128):
                        w = slice(c, c + 128)
                        tile = r + c // 128
                        g = jnp.concatenate([gs[i][tile], gs[i][tile + 8]], 0)
                        new = step_tile(g, *(x[there, w] for x in parts[:3]), rate)
                        for ref, value in zip(held, new):
                            ref[span, w] = value
                        held[3][span, w] = new[0].astype(bf16)
                for o in range(4):
                    copies.append(
                        pltpu.make_async_copy(
                            held[o].at[pl.ds(i * QUARTER, QUARTER)],
                            parts[3 + o].at[pl.ds(first, QUARTER)],
                            sem.at[i * 4 + o],
                        )
                    )
                    copies[-1].start()
            for copy in copies:
                copy.wait()

        scratch = [pltpu.VMEM((n * QUARTER, GATE), t) for t in kinds]
        scratch += [pltpu.SemaphoreType.DMA((4 * n,))]
        if few_too:
            scratch += [pltpu.VMEM(*x) for x in few_shapes]
            scratch += [pltpu.VMEM((96, 8, 128), f32), pltpu.SemaphoreType.DMA((8,))]
        result = call(
            body, f"{key}_update{n}" + ("_few" if few_too else ""), [*ins, *old],
            [(trio[0].shape, t) for t in kinds] + (few_shapes if few_too else []),
            specs=[VMEM] * len(ins) + [HBM] * len(old),
            out_specs=[HBM] * (12 if few_too else 4), scratch=scratch,
            aliases={len(ins) + i: i for i in range(len(old))},
        )
        state[key] = result[:4]
        if few_too:
            state["few"] = result[4:]

    def spread(total):
        while not total.done:
            total.advance()
        total.pieces = [total.piece, total.pairs.swap(total.piece, 0), total.pairs.swap(total.piece, 1)]

    def relay(total):
        total.pieces.append(total.pairs.swap(total.pieces[2], 0))

    trees = {"P": (proj_sum, "proj", None), "0": (tap0_sum, "conv", 0), "1": (tap1_sum, "conv", 1)}
    fill = {"back": back}
    for i in range(2):
        fill[f"mix{i}"] = lambda i=i: mix(i * HALF)
        fill[f"sg{i}"] = lambda i=i: signal_grad(i * HALF)
    for word in SCRIPT.split():
        if word in trees:
            trees[word][0].advance()
        elif word in fill:
            fill[word]()
        elif word[0] == "s":
            spread(trees[word[1]][0])
        elif word[0] == "r":
            relay(trees[word[1]][0])
        else:
            items, name = [], None
            for letter in word[1:]:
                if letter in trees:
                    name = letter
                elif letter in "abcd":
                    total, key, lead = trees[name]
                    items.append((total, "abcd".index(letter), lead))
            update(key, items, "f" in word)
    proj_new, conv_new = state["proj"], state["conv"]
    cond_new, bias_new = state["few"][:4], [x.reshape(-1) for x in state["few"][4:]]
    result = [*state["mixed"], *state["signal_grad"]]
    for k in range(4):
        result += [conv_new[k], cond_new[k], proj_new[k], bias_new[k]]
    return tuple(result)


WHOLE = (2, 1, 1)
SCRIPT = """
P sg0 P 1 back 0 mix0 P 1 mix1 0 1 P 0 1 P 0 1 0 sP rP 1 sg1 0 s0 1 s1 =0a =Pab r0 =Pd =Pc r1 =0cd1c =1b =0b1adf
"""


def shards(*args):
    return solve(Pairs("proj"), args)


def solution(mesh):
    rows = P(("blk", "seq"), None)
    in_specs = (rows, P(("blk", "seq")), P(("blk", "seq")), rows, rows, rows) + (P(),) * 12
    out_specs = (rows,) * 4 + (P(),) * 16
    return jax.shard_map(shards, mesh=mesh, in_specs=in_specs, out_specs=out_specs, check_vma=False)
```

```python
import math

import jax
import jax.numpy as jnp
from jax import lax
from jax.experimental import pallas as pl
from jax.experimental.pallas import tpu as pltpu
from jax.sharding import PartitionSpec as P

RESID = 512
GATE = 1024
MELS = 80
DILATION = 64
HALF = 512

f32 = jnp.float32
bf16 = jnp.bfloat16
momentum_rate = 0.9
ema_decay = 0.5
step_scale = 0.15
axes = ("blk", "seq")

VMEM = pl.BlockSpec(memory_space=pltpu.VMEM)
HBM = pl.BlockSpec(memory_space=pltpu.HBM)
ANY = pl.BlockSpec(memory_space=pl.ANY)
MIB = 1 << 20


TOKEN = ((8, 128), f32)

RATE = 2.9e9
TIMES = {
    "pack": 1, "late_gates": 4, "early_gates": 4.4, "gate_grad": 3.4, "proj_grad": 1.4, "tap0_grad": 1.4,
    "tap1_grad0": 2, "tap1_grad1": 1.4,
}
WORK = {"do": 0.7, "mix": 1.5, "sg": 2.8, "back": 0.5, "few": 0.8, "u1": 0.7, "u2": 1.3, "u3": 1.9, "u4": 2.5}
FOLD = 0.03


def expected(name):
    if name.startswith("do_"):
        return sum(WORK.get(word, 3) for word in name.split("_"))
    for key in sorted(TIMES, key=len, reverse=True):
        if key in name:
            return TIMES[key]
    return FOLD


class Order:
    def __init__(self):
        self.last = None

    def call(
        self, body, name, ins, outs, specs=None, out_specs=None, scratch=(), limit=16, aliases=None
    ):
        specs = list(specs) if specs else [VMEM] * len(ins)
        ins = [
            pltpu.with_memory_space_constraint(x, pltpu.HBM) if s is HBM else x
            for x, s in zip(ins, specs)
        ]
        out_specs = list(out_specs) if out_specs else [VMEM] * len(outs)
        after = [] if self.last is None else [self.last]
        n_in, n_after, n_out = len(ins), len(after), len(outs)

        def run(*refs):
            outs = refs[n_in + n_after : n_in + n_after + n_out]
            token = refs[n_in + n_after + n_out]
            token[...] = jnp.zeros(token.shape, f32)
            body(*refs[:n_in], *outs, *refs[n_in + n_after + n_out + 1 :])

        kinds = {id(VMEM): pltpu.VMEM, id(HBM): pltpu.HBM}
        *result, self.last = pl.pallas_call(
            run,
            out_shape=[kinds[id(s)](*o) for o, s in zip(outs, out_specs)] + [pltpu.VMEM(*TOKEN)],
            in_specs=specs + [VMEM] * n_after,
            out_specs=out_specs + [VMEM],
            scratch_shapes=list(scratch),
            input_output_aliases=aliases or {},
            compiler_params=pltpu.CompilerParams(vmem_limit_bytes=limit * MIB),
            cost_estimate=pl.CostEstimate(
                flops=int(RATE * expected(name)), bytes_accessed=1, transcendentals=0
            ),
            name=name,
        )(*ins, *after)
        return result


wide8 = jnp.float8_e5m2
fine8 = jnp.float8_e4m3fn
SIGNAL_SCALE, CONV_SCALE, GRAD_SCALE = 2.0**12, 2.0**18, 2.0**3
UP_SCALE, PROJ_SCALE, GATED_SCALE = 2.0**6, 2.0**9, 2.0**8
LOW = 256.0


def split(x):
    high = x.astype(bf16)
    return high, (x - high.astype(f32)).astype(bf16)


class Part:
    def __init__(self, name, ins, outs, start, done, old=(), scratch=(), to_hbm=True):
        self.name, self.ins, self.outs, self.start, self.done = name, list(ins), list(outs), start, done
        self.old, self.scratch, self.to_hbm = list(old), list(scratch), to_hbm


def run_parts(order, parts):
    ins, specs, outs, out_specs, scratch, aliases = [], [], [], [], [], {}
    for part in parts:
        for i in range(len(part.old)):
            aliases[len(ins) + len(part.ins) + i] = len(outs) + i
        ins += part.ins + part.old
        specs += [VMEM] * len(part.ins) + [HBM] * len(part.old)
        outs += part.outs
        out_specs += [HBM if part.to_hbm else VMEM] * len(part.outs)
        scratch += part.scratch
    n_in, n_out = len(ins), len(outs)

    def body(*refs):
        ins, outs, scratch = list(refs[:n_in]), list(refs[n_in : n_in + n_out]), list(refs[n_in + n_out :])
        copies = []
        for part in parts:
            mine = [ins.pop(0) for _ in part.ins]
            del ins[: len(part.old)]
            mine += [outs.pop(0) for _ in part.outs]
            mine += [scratch.pop(0) for _ in part.scratch]
            copies += part.start(*mine)
        for copy in copies:
            copy.wait()

    name = "_".join(["do"] + [part.name for part in parts])
    result = order.call(
        body, name, ins, outs, specs=specs, out_specs=out_specs, scratch=scratch, aliases=aliases, limit=20
    )
    for part in parts:
        part.done([result.pop(0) for _ in part.outs])


def put(refs, where, x, scale):
    high = x.astype(bf16)
    refs[0][where] = high
    refs[1][where] = (high * bf16(scale)).astype(refs[1].dtype)
    refs[2][where] = ((x - high.astype(f32)) * (scale * LOW)).astype(refs[2].dtype)


def dot(left, right, over):
    return lax.dot_general(left, right, (over, ((), ())), preferred_element_type=f32)


def product(left, right, over, scale):
    axis = [o[0] for o in over]
    low = jnp.concatenate([left[2], left[1]], axis[0])
    high = jnp.concatenate([right[1], right[2]], axis[1])
    return dot(left[0], right[0], over) + dot(low, high, over) * (1.0 / (LOW * scale))


def exact(left, right, over):
    return lax.dot_general(
        left, right, (over, ((), ())), preferred_element_type=f32, precision=lax.Precision.HIGHEST
    )


NN = ((1,), (0,))
NT = ((1,), (1,))
TN = ((0,), (0,))


ORDERS = {
    "proj": ((2, 1, 3, 4), (1, 2, 4, 3)),
    "tap0": ((2, 3, 1, 4), (1, 4, 2, 3)),
    "tap1": ((2, 1, 3, 4), (1, 2, 4, 3)),
}
LARGE = ((6, 0, 3, 7, 1, 4, 5), (0, 6, 3, 1, 7, 4, 5))


def plan(blk, seq, name):
    if (blk, seq) == (8, 4):
        return 0, ORDERS[name]
    if (blk, seq) == (64, 4):
        return 2, LARGE
    rest = tuple(range(1, (blk * seq).bit_length() - 1))
    return 0, (rest, rest)


class Pairs:
    def __init__(self, name):
        blk, seq = lax.axis_size("blk"), lax.axis_size("seq")
        self.count = blk * seq
        self.core_bit, (first, second) = plan(blk, seq, name)
        self.places = [(self.core_bit, self.core_bit), *zip(first, second)]
        self.steps = len(self.places)
        self.pairs = [
            [(i, i ^ (1 << p[(i >> self.core_bit) & 1])) for i in range(self.count)]
            for p in self.places
        ]

    def bit(self, step, sibling=False):
        me = lax.axis_index(axes)
        core = (me >> self.core_bit) & 1
        if sibling:
            core = 1 - core
        if step == 0:
            return core
        a, b = self.places[step]
        return jnp.where(core == 0, (me >> a) & 1, (me >> b) & 1)

    def quarter(self, k):
        core, bit = self.bit(0), self.bit(1, k % 2 == 1)
        return (1 - core if k % 2 else core) * 2 + (1 - bit if k >= 2 else bit)

    def swap(self, x, step):
        return lax.ppermute(x, axes, self.pairs[step])


class Sum:
    def __init__(self, order, pairs, name, send, whole=1):
        self.order, self.pairs, self.name = order, pairs, name
        self.parted = pairs.steps - whole
        self.step, self.back = 0, False
        self.got = pairs.swap(send, 0)
        self.done = False

    def advance(self):
        if self.done:
            return
        pairs, step = self.pairs, self.step
        label = f"{self.name}_{'join' if self.back else 'fold'}{step}"
        if self.back:
            size = self.piece.shape[0]

            def body(mine, got, out):
                bit = pairs.bit(step)
                out[pl.ds(bit * size, size)] = mine[...]
                out[pl.ds((1 - bit) * size, size)] = got[...]

            (self.piece,) = self.order.call(
                body, label, [self.piece, self.got], [((2 * size, 8, 128), f32)]
            )
            self.step -= 1
        elif step + 1 < self.parted:
            half = self.rest.shape[0] // 2

            def body(keep, got, send, rest):
                bit = pairs.bit(step + 1)
                here, there = pl.ds(bit * half, half), pl.ds((1 - bit) * half, half)
                send[...] = keep[there] + got[there]
                rest[...] = keep[here] + got[here]

            shape = ((half, 8, 128), f32)
            send, self.rest = self.order.call(body, label, [self.rest, self.got], [shape, shape])
            self.step += 1
            self.got = pairs.swap(send, self.step)
            return
        else:
            mine = self.rest if step < self.parted else self.piece

            def body(mine, got, out):
                out[...] = mine[...] + got[...]

            (self.piece,) = self.order.call(body, label, [mine, self.got], [(mine.shape, f32)])
            self.step += 1
            if self.step == pairs.steps:
                self.back, self.step = True, self.parted - 1
        if self.back and self.step == 1:
            self.done = True
            return
        self.got = pairs.swap(self.piece, self.step)


def pack_body(rows, signal, mel, out, frames, sem):
    copy = pltpu.make_async_copy(
        signal.at[pl.ds(rows - DILATION, DILATION)], out.at[pl.ds(0, DILATION)], sem.at[0]
    )
    other = pltpu.make_async_copy(mel, frames, sem.at[1])
    copy.start()
    other.start()
    out[DILATION:, :] = jnp.zeros((8, RESID), f32)
    other.wait()
    out[DILATION : DILATION + mel.shape[0], :MELS] = frames[...]
    copy.wait()


def columns(row, rows):
    return jnp.transpose(jnp.broadcast_to(row, (8, rows)))[:, :1]


def picks(slots, part, slot_count, sel):
    me = lax.axis_index(axes)
    local = (slots[:, part * HALF : (part + 1) * HALF] - (me - 1) * slot_count).astype(f32)
    local = columns(local, HALF).astype(jnp.int32)
    lane = lax.broadcasted_iota(jnp.int32, (HALF, 128), 1)
    hot = (lane == local) | (lane == local + 16) | (lane == 15)
    sel[...] = jnp.where(hot, 1.0, 0.0).astype(bf16)


def usable_row(starts, first, count, row_count):
    time = lax.axis_index(axes) * row_count + first + lax.broadcasted_iota(jnp.int32, (1, count), 1)
    return jnp.where(time - DILATION >= starts[:, first : first + count], 1.0, 0.0)


def frame_terms(mel, prior, cond, bias, table, frames):
    slot_count = mel.shape[0]
    frames[...] = jnp.zeros((16, 128), f32)
    frames[slot_count : 2 * slot_count, :MELS] = mel[...]
    if prior is not None:
        frames[:slot_count, :MELS] = prior
    row = jnp.concatenate([bias[i : i + 1, :] for i in range(8)], 1)
    terms = exact(frames[:, :MELS], cond[...], NN) + row
    keep = lax.broadcasted_iota(jnp.int32, (16, GATE), 0) < 2 * slot_count
    high, low = split(jnp.where(keep, terms, 0.0))
    table[...] = jnp.zeros((128, GATE), bf16)
    table[0:16, :] = high
    table[16:32, :] = low


def gates(tanh_in, sigm_in, cols, g, ca, cb):
    th = jnp.tanh(tanh_in)
    sg = 0.5 * jnp.tanh(0.5 * sigm_in) + 0.5
    gated = th * sg
    put(g, (slice(None), cols), gated, GATED_SCALE)
    ca[:, cols] = sg * (1.0 - th * th)
    cb[:, cols] = gated * (1.0 - sg)


def preact_block(d, x, sel, w, table, cols):
    main = dot(
        jnp.concatenate([d[0][...], x[0][...], sel[...]], 1),
        jnp.concatenate([w[0][:, cols], table[:, cols]], 0),
        NN,
    )
    low = dot(
        jnp.concatenate([d[2][...], x[2][...], d[1][...], x[1][...]], 1),
        jnp.concatenate([w[1][:, cols], w[2][:, cols]], 0),
        NN,
    )
    return main + low * (1.0 / (LOW * SIGNAL_SCALE * CONV_SCALE))


BLOCK = 256


def late_body(rows, *refs):
    signal, conv, cond, mel, slots, starts, bias = refs[:7]
    x0, x1, d, w = (refs[i : i + 3] for i in (7, 10, 13, 16))
    sel, g, ca, cb, table, frames = refs[19], refs[20:23], *refs[23:]
    first = HALF - DILATION
    picks(slots, 1, mel.shape[0], sel)
    frame_terms(mel, None, cond, bias, table, frames)
    usable = columns(usable_row(starts, HALF, HALF, rows), HALF)
    put(x1, slice(None), signal[HALF:, :], SIGNAL_SCALE)
    put(d, slice(None), signal[first : first + HALF, :] * usable, SIGNAL_SCALE)
    for j in range(HALF // BLOCK):
        blocks = [slice(c + j * BLOCK, c + (j + 1) * BLOCK) for c in (0, HALF)]
        products = []
        for cols in blocks:
            for tap in range(2):
                span = slice(tap * RESID, (tap + 1) * RESID)
                put(w, (span, cols), conv[tap, :, cols], CONV_SCALE)
            products.append(preact_block(d, x1, sel, w, table, cols))
        gates(*products, blocks[0], g, ca, cb)
    put(x0, slice(None), signal[0:HALF, :], SIGNAL_SCALE)


def early_body(rows, *refs):
    halo, signal = refs[:2]
    x, w = refs[2:5], refs[5:8]
    cond, mel, slots, starts, bias, resid_cotan, skip_cotan, proj = refs[8:16]
    d, sel, g, ca, cb = refs[16:19], refs[19], refs[20:23], refs[23], refs[24]
    u, p, usum, table, frames = refs[25:28], refs[28:31], *refs[31:]
    picks(slots, 0, mel.shape[0], sel)
    frame_terms(mel, halo[DILATION : DILATION + mel.shape[0], :MELS], cond, bias, table, frames)
    usable = columns(usable_row(starts, 0, HALF, rows), HALF)
    put(d, slice(0, DILATION), halo[0:DILATION, :] * usable[0:DILATION], SIGNAL_SCALE)
    rest = HALF - DILATION
    put(d, slice(DILATION, None), signal[0:rest, :] * usable[DILATION:], SIGNAL_SCALE)
    totals = [jnp.zeros((8, RESID), f32), jnp.zeros((8, RESID), f32)]

    def part_cotangents(first, count):
        for r in range(first, first + count, 32):
            for k, part in enumerate((resid_cotan, skip_cotan)):
                value = part[r : r + 32, :]
                put(u, (slice(r, r + 32), slice(k * RESID, (k + 1) * RESID)), value, UP_SCALE)
                totals[k] = totals[k] + jnp.sum(value.reshape(4, 8, RESID), 0)

    for r in range(0, HALF, 32):
        put(p, slice(r, r + 32), proj[r : r + 32, :], PROJ_SCALE)
    for j in range(HALF // BLOCK):
        tc, sc = (slice(c + j * BLOCK, c + (j + 1) * BLOCK) for c in (0, HALF))
        part_cotangents(j * rows // 2, rows // 4)
        tanh_in = preact_block(d, x, sel, w, table, tc)
        part_cotangents(j * rows // 2 + rows // 4, rows // 4)
        sigm_in = preact_block(d, x, sel, w, table, sc)
        gates(tanh_in, sigm_in, tc, g, ca, cb)
    usum[...] = jnp.concatenate(totals, 1)


def put_tiles(out, value, col0, stride=None):
    height, width = value.shape
    for r in range(height // 8):
        base = r * 8 if stride is None else (r * 8 // QUARTER) * stride + (r * 8) % QUARTER
        for c in range(width // 128):
            out[base + col0 // 128 + c] = value[8 * r : 8 * r + 8, 128 * c : 128 * c + 128]


WIDE = 512


def weight_grad(left, cols, right, out, scale, stride=None):
    left = [jnp.concatenate([a[:, cols], b[:, cols]], 0) for a, b in zip(left[:3], left[3:])]
    for c in range(0, GATE, WIDE):
        wide = [r[:, c : c + WIDE] for r in right]
        put_tiles(out, product(left, wide, TN, scale), c, stride)


QUARTER = 128


def solve(pairs, args):
    (
        signal, item_start, frame_slot, mel_frames, resid_cotan, skip_cotan,
        conv_weight, cond_weight, proj_weight, biases,
        conv_moment, cond_moment, proj_moment, biases_moment,
        conv_average, cond_average, proj_average, biases_average,
    ) = args
    rows = signal.shape[0]
    slot_count = mel_frames.shape[0]
    slots = frame_slot.reshape(1, rows)
    starts = item_start.reshape(1, rows)
    bias = biases.reshape(16, 128)
    count = pairs.count
    order = Order()
    call = order.call

    def core_half(own):
        bit = pairs.bit(0)
        return bit if own else 1 - bit

    def half_cols(own):
        return pl.ds(pl.multiple_of(core_half(own) * 2 * QUARTER, 2 * QUARTER), 2 * QUARTER)

    (packed,) = call(
        lambda *r: pack_body(rows, *r), "pack", [signal, mel_frames],
        [((DILATION + 8, RESID), f32)], specs=[HBM, HBM],
        scratch=[pltpu.VMEM((slot_count, MELS), f32), pltpu.SemaphoreType.DMA((2,))],
    )
    halo = lax.ppermute(packed, axes, [(i, i + 1) for i in range(count - 1)])

    wide, fine = (bf16, wide8, wide8), (bf16, fine8, fine8)
    half = [((HALF, RESID), t) for t in wide]
    half_gate = [((HALF, RESID), t) for t in fine]
    half32 = ((HALF, HALF), f32)
    square = [((GATE, GATE), t) for t in wide]
    pick = ((HALF, 128), bf16)
    small_scratch = [pltpu.VMEM((128, GATE), bf16), pltpu.VMEM((16, 128), f32)]
    out = call(
        lambda *r: late_body(rows, *r), "late_gates",
        [signal, conv_weight, cond_weight, mel_frames, slots, starts, bias],
        [*half, *half, *half, *square, pick, *half_gate, half32, half32], scratch=small_scratch,
    )
    x0, x1, d1, w = (out[i : i + 3] for i in (0, 3, 6, 9))
    sel1, g1, ca1, cb1 = out[12], out[13:16], out[16], out[17]
    out = call(
        lambda *r: early_body(rows, *r), "early_gates",
        [halo, signal, *x0, *w, cond_weight, mel_frames, slots, starts, bias,
         resid_cotan, skip_cotan, proj_weight],
        [*half, pick, *half_gate, half32, half32, *(((GATE, GATE), t) for t in fine),
         *(((HALF, GATE), t) for t in fine), ((8, GATE), f32)],
        scratch=small_scratch,
    )
    d0, sel0, g0, ca0, cb0 = out[0:3], out[3], out[4:7], out[7], out[8]
    u, p, usum = out[9:12], out[12:15], out[15]

    tiles = ((2 * QUARTER, 8, 128), f32)
    few = 24
    while (QUARTER + few) % max(1, count // 4):
        few += 8
    quarter = QUARTER + few
    wide_tiles = ((2 * quarter, 8, 128), f32)
    state = {}
    sums = {}

    def grad_half(own, scale, stride=None):
        def body(*refs):
            weight_grad(refs[:6], half_cols(own), refs[6:9], refs[9], scale, stride)

        return body

    def proj_grad(own):
        body = grad_half(own, GATED_SCALE * UP_SCALE)
        (out,) = call(body, f"proj_grad{own:d}", [*g0, *g1, *u], [tiles])
        return out

    def tap0_grad(own):
        body = grad_half(own, SIGNAL_SCALE * GRAD_SCALE)
        (out,) = call(body, f"tap0_grad{own:d}", [*d0, *d1, *state["gp"]], [tiles])
        return out

    def tap1_half(own, *refs):
        both, out = refs[9:]
        grad_half(own, SIGNAL_SCALE * GRAD_SCALE, quarter)(*refs[:9], out)
        for q in range(2):
            out[pl.ds(q * quarter + QUARTER, few)] = both[core_half(own) * 2 + q]

    def tap1_first(*refs):
        x, gp, (sel0, sel1, usum, mel, halo) = refs[:6], refs[6:9], refs[9:14]
        out, both, frame_grad, frames = refs[14:]
        sel = jnp.concatenate([sel0[:, 0:16], sel1[:, 0:16]], 0)
        found = dot(sel, gp[0][...], TN)
        found += dot(sel.astype(wide8), gp[2][...], TN) * (1.0 / (LOW * GRAD_SCALE))
        frame_grad[...] = found
        frames[...] = jnp.zeros((16, 128), f32)
        frames[:slot_count, :MELS] = halo[DILATION : DILATION + slot_count, :MELS]
        frames[slot_count : 2 * slot_count, :MELS] = mel[...]
        cond_grad = exact(frames[:, :MELS], found, TN)
        both[...] = jnp.zeros((4, few, 8, 128), f32)
        for q in range(4):
            part = cond_grad[24 * q : min(24 * q + 24, MELS), :]
            put_tiles(both.at[q], part, 0)
        sums = jnp.sum(usum[...], 0, keepdims=True)
        for i in range(8):
            lane = slice(128 * i, 128 * i + 128)
            both[3, 8, i : i + 1, :] = found[15:16, lane]
            both[3, 9, i : i + 1, :] = sums[:, lane]
        tap1_half(False, *x, *gp, both, out)

    def tap1_grad(own):
        ins = [*x0, *x1, *state["gp"]]
        if own:
            (out,) = call(
                lambda *r: tap1_half(True, *r), "tap1_grad1", [*ins, state["few_grad"]], [wide_tiles]
            )
            return out
        out, state["few_grad"], state["frame_grad"] = call(
            tap1_first, "tap1_grad0", [*ins, sel0, sel1, usum, mel_frames, halo],
            [wide_tiles, ((4, few, 8, 128), f32), ((16, GATE), f32)],
            scratch=[pltpu.VMEM((16, 128), f32)],
        )
        return out

    def gate_grad():
        def body(*refs):
            u, p, (ca0, ca1, cb0, cb1), gp = refs[:3], refs[3:6], refs[6:10], refs[10:]
            right = [x[...] for x in p]
            for r in range(0, rows, BLOCK):
                span = slice(r, r + BLOCK)
                grad = product([x[span, :] for x in u], right, NT, UP_SCALE * PROJ_SCALE)
                ca, cb = (ca0, cb0) if r < HALF else (ca1, cb1)
                inner = slice(r % HALF, r % HALF + BLOCK)
                put(gp, (span, slice(0, HALF)), grad * ca[inner, :], GRAD_SCALE)
                put(gp, (span, slice(HALF, GATE)), grad * cb[inner, :], GRAD_SCALE)

        state["gp"] = call(body, "gate_grad", [*u, *p, ca0, ca1, cb0, cb1], square)

    grads = {"P": ("proj", proj_grad), "0": ("tap0", tap0_grad), "1": ("tap1", tap1_grad)}

    def first_half(key):
        name, grad = grads[key]
        whole = WHOLE["P01".index(key)]
        sums[key] = Sum(order, Pairs(name), name, grad(False), whole)

    def second_half(key):
        sums[key].rest = grads[key][1](True)

    def tap_back(gp, w, rows_, tap):
        span = slice(tap * RESID, (tap + 1) * RESID)
        return product(
            [x[rows_, :] for x in gp], [x[span, :] for x in w], NT, GRAD_SCALE * CONV_SCALE
        )

    def back_body(*refs):
        gp, w, (frame_grad, cond, starts, out, own) = refs[:3], refs[3:6], refs[6:]
        usable = columns(usable_row(starts, 0, 128, rows), 128)[0:DILATION]
        out[0:DILATION, :] = tap_back(gp, w, slice(0, DILATION), 0) * usable
        mels = exact(frame_grad[...], cond[...], NT)
        out[DILATION:, :] = jnp.zeros((8, RESID), f32)
        out[DILATION : DILATION + slot_count, :MELS] = mels[:slot_count]
        own[...] = mels[slot_count : 2 * slot_count]
        return []

    def back():
        def done(result):
            state["mel_own"] = result[1]
            state["came"] = lax.ppermute(result[0], axes, [(i, i - 1) for i in range(1, count)])

        return Part(
            "back", [*state["gp"], *w, state["frame_grad"], cond_weight, starts],
            [((DILATION + 8, RESID), f32), ((slot_count, MELS), f32)], back_body, done, to_hbm=False,
        )

    def mix(r):
        def start(*refs):
            g, p, (bias, signal) = refs[:3], refs[3:6], refs[6:8]
            outs, (held, sem) = refs[8:10], refs[10:]
            copies = []
            for s in range(0, HALF, BLOCK):
                inner = slice(s, s + BLOCK)
                span = slice(r + s, r + s + BLOCK)
                left = [x[inner, :] for x in g]
                for k, c in enumerate((0, RESID)):
                    w = slice(c, c + RESID)
                    first = 8 + c // 128
                    row = jnp.concatenate([bias[i : i + 1, :] for i in range(first, first + 4)], 1)
                    mixed = product(left, [x[:, w] for x in p], NN, GATED_SCALE * PROJ_SCALE) + row
                    held[k, inner, :] = mixed + signal[span, :] if k == 0 else mixed
                    copies.append(
                        pltpu.make_async_copy(
                            held.at[k, pl.ds(s, BLOCK)],
                            outs[k].at[pl.ds(r + s, BLOCK)],
                            sem.at[len(copies)],
                        )
                    )
                    copies[-1].start()
            return copies

        return Part(
            "mix", [*(g0 if r < HALF else g1), *p, bias, signal], [((rows, RESID), f32)] * 2,
            start, lambda result: state.update(mixed=result), old=state.get("mixed", ()),
            scratch=[pltpu.VMEM((2, HALF, RESID), f32), pltpu.SemaphoreType.DMA((4,))],
        )

    def signal_grad(r):
        last = r + HALF == rows

        def start(*refs):
            gp, w, (starts, resid_cotan) = refs[:3], refs[3:6], refs[6:8]
            held, mels, sem = refs[-3:]
            copies = []
            if last:
                came, own, out, mel_grad = refs[8:-3]
                mels[...] = own[...] + came[DILATION : DILATION + slot_count, :MELS]
                copies.append(pltpu.make_async_copy(mels, mel_grad, sem.at[2]))
                copies[0].start()
            else:
                out = refs[8]
            usable = columns(usable_row(starts, 0, rows, rows), rows)
            for s in range(r, r + HALF, BLOCK):
                span = slice(s, s + BLOCK)
                ahead = slice(s + DILATION, min(s + DILATION + BLOCK, rows))
                inner = slice(s - r, s - r + BLOCK)
                later = tap_back(gp, w, ahead, 0) * usable[ahead]
                held[inner, :] = tap_back(gp, w, span, 1) + resid_cotan[span, :]
                held[s - r : s - r + later.shape[0], :] += later
                if s + BLOCK == rows:
                    held[HALF - DILATION :, :] += came[0:DILATION, :]
                copies.append(
                    pltpu.make_async_copy(
                        held.at[pl.ds(s - r, BLOCK)], out.at[pl.ds(s, BLOCK)], sem.at[(s - r) // BLOCK]
                    )
                )
                copies[-1].start()
            return copies

        ins = [*state["gp"], *w, starts, resid_cotan]
        outs = [((rows, RESID), f32)]
        if last:
            ins += [state["came"], state["mel_own"]]
            outs += [((slot_count, MELS), f32)]
        return Part(
            "sg", ins, outs, start, lambda result: state.update(signal_grad=result),
            old=state.get("signal_grad", ()),
            scratch=[pltpu.VMEM((HALF, RESID), f32), pltpu.VMEM((slot_count, MELS), f32),
                     pltpu.SemaphoreType.DMA((3,))],
        )

    root = math.sqrt(rows * count)
    conv_rate = step_scale / (math.sqrt(2 * RESID) * 1.5 * root)
    cond_rate = step_scale / (math.sqrt(MELS) * 1.5 * root)
    proj_rate = step_scale / (math.sqrt(GATE // 16) * 0.3 * root)
    biases_rate = step_scale * 0.3 / (1.2 * root)

    def step_tile(g, w, m, a, rate):
        m = momentum_rate * m + g
        w = w - rate * (g + momentum_rate * m)
        return w, m, ema_decay * a + (1.0 - ema_decay) * w

    conv = (conv_weight, conv_moment, conv_average)
    matrices = {
        "proj": ((proj_weight, proj_moment, proj_average), proj_rate),
        "conv": (conv, conv_rate),
    }
    kinds = (f32, f32, f32, bf16)
    few_args = (cond_weight, cond_moment, cond_average, bias,
                biases_moment.reshape(16, 128), biases_average.reshape(16, 128))
    few_shapes = [((MELS, GATE), t) for t in kinds] + [((16, 128), t) for t in kinds]

    def update_few(pieces, ins, outs, held, grads, sem):
        for k, piece in enumerate(pieces):
            first = sums["1"].pairs.quarter(k) * 24
            grads[pl.ds(first, 24)] = piece[QUARTER : QUARTER + 24]
        for r in range(0, MELS, 16):
            span = slice(r, r + 16)
            for c in range(0, GATE, 128):
                w = slice(c, c + 128)
                tile = r + c // 128
                g = jnp.concatenate([grads[tile], grads[tile + 8]], 0)
                new = step_tile(g, *(x[span, w] for x in ins[:3]), cond_rate)
                for ref, value in zip(held, new):
                    ref[span, w] = value
                held[3][span, w] = new[0].astype(bf16)
        grad = jnp.concatenate([grads[MELS], grads[MELS + 1]], 0)
        new = step_tile(grad, *(x[...] for x in ins[3:]), biases_rate)
        for ref, value in zip(held[4:], new):
            ref[...] = value
        held[7][...] = new[0].astype(bf16)
        copies = [
            pltpu.make_async_copy(a, b, sem.at[i]) for i, (a, b) in enumerate(zip(held, outs))
        ]
        for copy in copies:
            copy.start()
        return copies

    def update(key, items):
        trio, rate = matrices[key]
        n = len(items)

        def start(*refs):
            gs, trio_refs, outs = refs[:n], refs[n : n + 3], refs[n + 3 : n + 7]
            held, sem = refs[n + 7 : n + 11], refs[n + 11]
            copies = []
            for i, (total, k, lead) in enumerate(items):
                first = pl.multiple_of(total.pairs.quarter(k) * QUARTER, QUARTER)
                parts = [x if lead is None else x.at[lead] for x in (*trio_refs, *outs)]
                for r in range(0, QUARTER, 16):
                    span = slice(i * QUARTER + r, i * QUARTER + r + 16)
                    there = pl.ds(first + r, 16)
                    for c in range(0, GATE, 128):
                        w = slice(c, c + 128)
                        tile = r + c // 128
                        g = jnp.concatenate([gs[i][tile], gs[i][tile + 8]], 0)
                        new = step_tile(g, *(x[there, w] for x in parts[:3]), rate)
                        for ref, value in zip(held, new):
                            ref[span, w] = value
                        held[3][span, w] = new[0].astype(bf16)
                for o in range(4):
                    copies.append(
                        pltpu.make_async_copy(
                            held[o].at[pl.ds(i * QUARTER, QUARTER)],
                            parts[3 + o].at[pl.ds(first, QUARTER)],
                            sem.at[i * 4 + o],
                        )
                    )
                    copies[-1].start()
            return copies

        return Part(
            f"u{n}", [total.pieces[k] for total, k, _ in items] + [*trio],
            [(trio[0].shape, t) for t in kinds], start,
            lambda result: state.update({key: result}), old=state.get(key, ()),
            scratch=[pltpu.VMEM((n * QUARTER, GATE), t) for t in kinds]
            + [pltpu.SemaphoreType.DMA((4 * n,))],
        )

    def few_update():
        def start(*refs):
            return update_few(refs[:4], refs[4:10], refs[10:18], refs[18:26], refs[26], refs[27])

        return Part(
            "few", [*sums["1"].pieces, *few_args], few_shapes, start,
            lambda result: state.update(few=result),
            scratch=[pltpu.VMEM(*x) for x in few_shapes]
            + [pltpu.VMEM((96, 8, 128), f32), pltpu.SemaphoreType.DMA((8,))],
        )

    def spread(key):
        total = sums[key]
        while not total.done:
            total.advance()
        total.pieces = [total.piece, total.pairs.swap(total.piece, 0), total.pairs.swap(total.piece, 1)]

    def relay(key):
        total = sums[key]
        total.pieces.append(total.pairs.swap(total.pieces[2], 0))

    owners = {"P": ("proj", None), "0": ("conv", 0), "1": ("conv", 1)}
    fill = {"back": back}
    for i in range(2):
        fill[f"mix{i}"] = lambda i=i: mix(i * HALF)
        fill[f"sg{i}"] = lambda i=i: signal_grad(i * HALF)

    def updates(word):
        named = {}
        for letter in word[1:]:
            if letter in owners:
                key, lead = owners[letter]
                total = sums[letter]
            elif letter in "abcd":
                named.setdefault(key, []).append((total, "abcd".index(letter), lead))
        return [update(key, items) for key, items in named.items()] + (
            [few_update()] if "f" in word else []
        )

    for word in SCRIPT.split():
        if word in owners:
            sums[word].advance()
        elif word == "gg":
            gate_grad()
        elif len(word) == 2 and word[0] in "jksr":
            {"j": first_half, "k": second_half, "s": spread, "r": relay}[word[0]](word[1])
        else:
            work = []
            for item in word.split("+"):
                work += updates(item) if item[0] == "=" else [fill[item]()]
            run_parts(order, work)
    proj_new, conv_new = state["proj"], state["conv"]
    cond_new, bias_new = state["few"][:4], [x.reshape(-1) for x in state["few"][4:]]
    result = [*state["mixed"], *state["signal_grad"]]
    for k in range(4):
        result += [conv_new[k], cond_new[k], proj_new[k], bias_new[k]]
    return tuple(result)


WHOLE = (2, 1, 1)
SCRIPT = """
jP gg kP P j0 k0 j1 k1 P 0 sg0 P 1 back 0 mix0 P 1 mix1 0 1 P 0 1 0 P 1 0 sP rP sg1 1 0 s0 =Pab 1 s1 r0 =Pd0a
r1 =0cd1bc =0b1adPcf
"""


def shards(*args):
    return solve(Pairs("proj"), args)


def solution(mesh):
    rows = P(("blk", "seq"), None)
    in_specs = (rows, P(("blk", "seq")), P(("blk", "seq")), rows, rows, rows) + (P(),) * 12
    out_specs = (rows,) * 4 + (P(),) * 16
    return jax.shard_map(shards, mesh=mesh, in_specs=in_specs, out_specs=out_specs, check_vma=False)
```

```python
import math

import jax
import jax.numpy as jnp
from jax import lax
from jax.experimental import pallas as pl
from jax.experimental.pallas import tpu as pltpu
from jax.sharding import PartitionSpec as P

RESID = 512
GATE = 1024
MELS = 80
DILATION = 64
HALF = 512

f32 = jnp.float32
bf16 = jnp.bfloat16
momentum_rate = 0.9
ema_decay = 0.5
step_scale = 0.15
axes = ("blk", "seq")

VMEM = pl.BlockSpec(memory_space=pltpu.VMEM)
HBM = pl.BlockSpec(memory_space=pltpu.HBM)
ANY = pl.BlockSpec(memory_space=pl.ANY)
MIB = 1 << 20


TOKEN = ((8, 128), f32)

RATE = 2.9e9
TIMES = {
    "pack": 1, "late_gates": 4, "early_gates": 4.4, "gate_grad": 3.4, "proj_grad": 1.4, "tap0_grad": 1.4,
    "tap1_grad0": 2, "tap1_grad1": 1.4,
}
WORK = {"do": 0.7, "mix": 1.5, "sg": 2.8, "back": 0.5, "few": 0.8, "u1": 0.7, "u2": 1.3, "u3": 1.9, "u4": 2.5}
FOLD = 0.03


def expected(name):
    if name.startswith("do_"):
        return sum(WORK.get(word, 3) for word in name.split("_"))
    for key in sorted(TIMES, key=len, reverse=True):
        if key in name:
            return TIMES[key]
    return FOLD


class Order:
    def __init__(self):
        self.last = None

    def call(
        self, body, name, ins, outs, specs=None, out_specs=None, scratch=(), limit=16, aliases=None
    ):
        specs = list(specs) if specs else [VMEM] * len(ins)
        ins = [
            pltpu.with_memory_space_constraint(x, pltpu.HBM) if s is HBM else x
            for x, s in zip(ins, specs)
        ]
        out_specs = list(out_specs) if out_specs else [VMEM] * len(outs)
        after = [] if self.last is None else [self.last]
        n_in, n_after, n_out = len(ins), len(after), len(outs)

        def run(*refs):
            outs = refs[n_in + n_after : n_in + n_after + n_out]
            token = refs[n_in + n_after + n_out]
            token[...] = jnp.zeros(token.shape, f32)
            body(*refs[:n_in], *outs, *refs[n_in + n_after + n_out + 1 :])

        kinds = {id(VMEM): pltpu.VMEM, id(HBM): pltpu.HBM}
        *result, self.last = pl.pallas_call(
            run,
            out_shape=[kinds[id(s)](*o) for o, s in zip(outs, out_specs)] + [pltpu.VMEM(*TOKEN)],
            in_specs=specs + [VMEM] * n_after,
            out_specs=out_specs + [VMEM],
            scratch_shapes=list(scratch),
            input_output_aliases=aliases or {},
            compiler_params=pltpu.CompilerParams(vmem_limit_bytes=limit * MIB),
            cost_estimate=pl.CostEstimate(
                flops=int(RATE * expected(name)), bytes_accessed=1, transcendentals=0
            ),
            name=name,
        )(*ins, *after)
        return result


wide8 = jnp.float8_e5m2
fine8 = jnp.float8_e4m3fn
SIGNAL_SCALE, CONV_SCALE, GRAD_SCALE = 2.0**12, 2.0**18, 2.0**3
UP_SCALE, PROJ_SCALE, GATED_SCALE = 2.0**6, 2.0**9, 2.0**8
LOW = 256.0


def split(x):
    high = x.astype(bf16)
    return high, (x - high.astype(f32)).astype(bf16)


class Part:
    def __init__(self, name, ins, outs, start, done, old=(), scratch=(), to_hbm=True):
        self.name, self.ins, self.outs, self.start, self.done = name, list(ins), list(outs), start, done
        self.old, self.scratch, self.to_hbm = list(old), list(scratch), to_hbm


def run_parts(order, parts):
    ins, specs, outs, out_specs, scratch, aliases = [], [], [], [], [], {}
    for part in parts:
        for i in range(len(part.old)):
            aliases[len(ins) + len(part.ins) + i] = len(outs) + i
        ins += part.ins + part.old
        specs += [VMEM] * len(part.ins) + [HBM] * len(part.old)
        outs += part.outs
        out_specs += [HBM if part.to_hbm else VMEM] * len(part.outs)
        scratch += part.scratch
    n_in, n_out = len(ins), len(outs)

    def body(*refs):
        ins, outs, scratch = list(refs[:n_in]), list(refs[n_in : n_in + n_out]), list(refs[n_in + n_out :])
        copies = []
        for part in parts:
            mine = [ins.pop(0) for _ in part.ins]
            del ins[: len(part.old)]
            mine += [outs.pop(0) for _ in part.outs]
            mine += [scratch.pop(0) for _ in part.scratch]
            copies += part.start(*mine)
        for copy in copies:
            copy.wait()

    name = "_".join(["do"] + [part.name for part in parts])
    result = order.call(
        body, name, ins, outs, specs=specs, out_specs=out_specs, scratch=scratch, aliases=aliases, limit=20
    )
    for part in parts:
        part.done([result.pop(0) for _ in part.outs])


def put(refs, where, x, scale):
    high = x.astype(bf16)
    refs[0][where] = high
    refs[1][where] = (high * bf16(scale)).astype(refs[1].dtype)
    refs[2][where] = ((x - high.astype(f32)) * (scale * LOW)).astype(refs[2].dtype)


def dot(left, right, over):
    return lax.dot_general(left, right, (over, ((), ())), preferred_element_type=f32)


def product(left, right, over, scale):
    axis = [o[0] for o in over]
    low = jnp.concatenate([left[2], left[1]], axis[0])
    high = jnp.concatenate([right[1], right[2]], axis[1])
    return dot(left[0], right[0], over) + dot(low, high, over) * (1.0 / (LOW * scale))


def exact(left, right, over):
    return lax.dot_general(
        left, right, (over, ((), ())), preferred_element_type=f32, precision=lax.Precision.HIGHEST
    )


NN = ((1,), (0,))
NT = ((1,), (1,))
TN = ((0,), (0,))


ORDERS = {
    "proj": ((2, 1, 3, 4), (1, 2, 4, 3)),
    "tap0": ((2, 3, 1, 4), (1, 4, 2, 3)),
    "tap1": ((2, 1, 3, 4), (1, 2, 4, 3)),
}
LARGE = ((6, 0, 3, 7, 1, 4, 5), (0, 6, 3, 1, 7, 4, 5))


def plan(blk, seq, name):
    if (blk, seq) == (8, 4):
        return 0, ORDERS[name]
    if (blk, seq) == (64, 4):
        return 2, LARGE
    rest = tuple(range(1, (blk * seq).bit_length() - 1))
    return 0, (rest, rest)


class Pairs:
    def __init__(self, name):
        blk, seq = lax.axis_size("blk"), lax.axis_size("seq")
        self.count = blk * seq
        self.core_bit, (first, second) = plan(blk, seq, name)
        self.places = [(self.core_bit, self.core_bit), *zip(first, second)]
        self.steps = len(self.places)
        self.pairs = [
            [(i, i ^ (1 << p[(i >> self.core_bit) & 1])) for i in range(self.count)]
            for p in self.places
        ]

    def bit(self, step, sibling=False):
        me = lax.axis_index(axes)
        core = (me >> self.core_bit) & 1
        if sibling:
            core = 1 - core
        if step == 0:
            return core
        a, b = self.places[step]
        return jnp.where(core == 0, (me >> a) & 1, (me >> b) & 1)

    def quarter(self, k):
        core, bit = self.bit(0), self.bit(1, k % 2 == 1)
        return (1 - core if k % 2 else core) * 2 + (1 - bit if k >= 2 else bit)

    def swap(self, x, step):
        return lax.ppermute(x, axes, self.pairs[step])


class Sum:
    def __init__(self, order, pairs, name, send, whole=1):
        self.order, self.pairs, self.name = order, pairs, name
        self.parted = pairs.steps - whole
        self.step, self.back = 0, False
        self.got = pairs.swap(send, 0)
        self.done = False

    def advance(self):
        if self.done:
            return
        pairs, step = self.pairs, self.step
        label = f"{self.name}_{'join' if self.back else 'fold'}{step}"
        if self.back:
            size = self.piece.shape[0]

            def body(mine, got, out):
                bit = pairs.bit(step)
                out[pl.ds(bit * size, size)] = mine[...]
                out[pl.ds((1 - bit) * size, size)] = got[...]

            (self.piece,) = self.order.call(
                body, label, [self.piece, self.got], [((2 * size, 8, 128), f32)]
            )
            self.step -= 1
        elif step + 1 < self.parted:
            half = self.rest.shape[0] // 2

            def body(keep, got, send, rest):
                bit = pairs.bit(step + 1)
                here, there = pl.ds(bit * half, half), pl.ds((1 - bit) * half, half)
                send[...] = keep[there] + got[there]
                rest[...] = keep[here] + got[here]

            shape = ((half, 8, 128), f32)
            send, self.rest = self.order.call(body, label, [self.rest, self.got], [shape, shape])
            self.step += 1
            self.got = pairs.swap(send, self.step)
            return
        else:
            mine = self.rest if step < self.parted else self.piece

            def body(mine, got, out):
                out[...] = mine[...] + got[...]

            (self.piece,) = self.order.call(body, label, [mine, self.got], [(mine.shape, f32)])
            self.step += 1
            if self.step == pairs.steps:
                self.back, self.step = True, self.parted - 1
        if self.back and self.step == 1:
            self.done = True
            return
        self.got = pairs.swap(self.piece, self.step)


def pack_body(rows, signal, mel, out, frames, sem):
    copy = pltpu.make_async_copy(
        signal.at[pl.ds(rows - DILATION, DILATION)], out.at[pl.ds(0, DILATION)], sem.at[0]
    )
    other = pltpu.make_async_copy(mel, frames, sem.at[1])
    copy.start()
    other.start()
    out[DILATION:, :] = jnp.zeros((8, RESID), f32)
    other.wait()
    out[DILATION : DILATION + mel.shape[0], :MELS] = frames[...]
    copy.wait()


def columns(row, rows):
    return jnp.transpose(jnp.broadcast_to(row, (8, rows)))[:, :1]


def picks(slots, part, slot_count, sel):
    me = lax.axis_index(axes)
    local = (slots[:, part * HALF : (part + 1) * HALF] - (me - 1) * slot_count).astype(f32)
    local = columns(local, HALF).astype(jnp.int32)
    lane = lax.broadcasted_iota(jnp.int32, (HALF, 128), 1)
    hot = (lane == local) | (lane == local + 16) | (lane == 15)
    sel[...] = jnp.where(hot, 1.0, 0.0).astype(bf16)


def usable_row(starts, first, count, row_count):
    time = lax.axis_index(axes) * row_count + first + lax.broadcasted_iota(jnp.int32, (1, count), 1)
    return jnp.where(time - DILATION >= starts[:, first : first + count], 1.0, 0.0)


def frame_terms(mel, prior, cond, bias, table, frames):
    slot_count = mel.shape[0]
    frames[...] = jnp.zeros((16, 128), f32)
    frames[slot_count : 2 * slot_count, :MELS] = mel[...]
    if prior is not None:
        frames[:slot_count, :MELS] = prior
    row = jnp.concatenate([bias[i : i + 1, :] for i in range(8)], 1)
    terms = exact(frames[:, :MELS], cond[...], NN) + row
    keep = lax.broadcasted_iota(jnp.int32, (16, GATE), 0) < 2 * slot_count
    high, low = split(jnp.where(keep, terms, 0.0))
    table[...] = jnp.zeros((128, GATE), bf16)
    table[0:16, :] = high
    table[16:32, :] = low


def gates(tanh_in, sigm_in, cols, g, ca, cb):
    th = jnp.tanh(tanh_in)
    sg = 0.5 * jnp.tanh(0.5 * sigm_in) + 0.5
    gated = th * sg
    put(g, (slice(None), cols), gated, GATED_SCALE)
    ca[:, cols] = sg * (1.0 - th * th)
    cb[:, cols] = gated * (1.0 - sg)


def preact_block(d, x, sel, w, table, cols):
    main = dot(
        jnp.concatenate([d[0][...], x[0][...], sel[...]], 1),
        jnp.concatenate([w[0][:, cols], table[:, cols]], 0),
        NN,
    )
    low = dot(
        jnp.concatenate([d[2][...], x[2][...], d[1][...], x[1][...]], 1),
        jnp.concatenate([w[1][:, cols], w[2][:, cols]], 0),
        NN,
    )
    return main + low * (1.0 / (LOW * SIGNAL_SCALE * CONV_SCALE))


BLOCK = 256


def late_body(rows, *refs):
    signal, conv, cond, mel, slots, starts, bias = refs[:7]
    x0, x1, d, w = (refs[i : i + 3] for i in (7, 10, 13, 16))
    sel, g, ca, cb, table, frames = refs[19], refs[20:23], *refs[23:]
    first = HALF - DILATION
    picks(slots, 1, mel.shape[0], sel)
    frame_terms(mel, None, cond, bias, table, frames)
    usable = columns(usable_row(starts, HALF, HALF, rows), HALF)
    put(x1, slice(None), signal[HALF:, :], SIGNAL_SCALE)
    put(d, slice(None), signal[first : first + HALF, :] * usable, SIGNAL_SCALE)
    for j in range(HALF // BLOCK):
        blocks = [slice(c + j * BLOCK, c + (j + 1) * BLOCK) for c in (0, HALF)]
        products = []
        for cols in blocks:
            for tap in range(2):
                span = slice(tap * RESID, (tap + 1) * RESID)
                put(w, (span, cols), conv[tap, :, cols], CONV_SCALE)
            products.append(preact_block(d, x1, sel, w, table, cols))
        gates(*products, blocks[0], g, ca, cb)
    put(x0, slice(None), signal[0:HALF, :], SIGNAL_SCALE)


def early_body(rows, *refs):
    halo, signal = refs[:2]
    x, w = refs[2:5], refs[5:8]
    cond, mel, slots, starts, bias, resid_cotan, skip_cotan, proj = refs[8:16]
    d, sel, g, ca, cb = refs[16:19], refs[19], refs[20:23], refs[23], refs[24]
    u, p, usum, table, frames = refs[25:28], refs[28:31], *refs[31:]
    picks(slots, 0, mel.shape[0], sel)
    frame_terms(mel, halo[DILATION : DILATION + mel.shape[0], :MELS], cond, bias, table, frames)
    usable = columns(usable_row(starts, 0, HALF, rows), HALF)
    put(d, slice(0, DILATION), halo[0:DILATION, :] * usable[0:DILATION], SIGNAL_SCALE)
    rest = HALF - DILATION
    put(d, slice(DILATION, None), signal[0:rest, :] * usable[DILATION:], SIGNAL_SCALE)
    totals = [jnp.zeros((8, RESID), f32), jnp.zeros((8, RESID), f32)]

    def part_cotangents(first, count):
        for r in range(first, first + count, 32):
            for k, part in enumerate((resid_cotan, skip_cotan)):
                value = part[r : r + 32, :]
                put(u, (slice(r, r + 32), slice(k * RESID, (k + 1) * RESID)), value, UP_SCALE)
                totals[k] = totals[k] + jnp.sum(value.reshape(4, 8, RESID), 0)

    for r in range(0, HALF, 32):
        put(p, slice(r, r + 32), proj[r : r + 32, :], PROJ_SCALE)
    for j in range(HALF // BLOCK):
        tc, sc = (slice(c + j * BLOCK, c + (j + 1) * BLOCK) for c in (0, HALF))
        part_cotangents(j * rows // 2, rows // 4)
        tanh_in = preact_block(d, x, sel, w, table, tc)
        part_cotangents(j * rows // 2 + rows // 4, rows // 4)
        sigm_in = preact_block(d, x, sel, w, table, sc)
        gates(tanh_in, sigm_in, tc, g, ca, cb)
    usum[...] = jnp.concatenate(totals, 1)


def put_tiles(out, value, col0, stride=None):
    height, width = value.shape
    for r in range(height // 8):
        base = r * 8 if stride is None else (r * 8 // QUARTER) * stride + (r * 8) % QUARTER
        for c in range(width // 128):
            out[base + col0 // 128 + c] = value[8 * r : 8 * r + 8, 128 * c : 128 * c + 128]


WIDE = 512


def weight_grad(left, cols, right, out, scale, stride=None):
    left = [jnp.concatenate([a[:, cols], b[:, cols]], 0) for a, b in zip(left[:3], left[3:])]
    for c in range(0, GATE, WIDE):
        wide = [r[:, c : c + WIDE] for r in right]
        put_tiles(out, product(left, wide, TN, scale), c, stride)


QUARTER = 128


def solve(pairs, args):
    (
        signal, item_start, frame_slot, mel_frames, resid_cotan, skip_cotan,
        conv_weight, cond_weight, proj_weight, biases,
        conv_moment, cond_moment, proj_moment, biases_moment,
        conv_average, cond_average, proj_average, biases_average,
    ) = args
    rows = signal.shape[0]
    slot_count = mel_frames.shape[0]
    slots = frame_slot.reshape(1, rows)
    starts = item_start.reshape(1, rows)
    bias = biases.reshape(16, 128)
    count = pairs.count
    order = Order()
    call = order.call

    def core_half(own):
        bit = pairs.bit(0)
        return bit if own else 1 - bit

    def half_cols(own):
        return pl.ds(pl.multiple_of(core_half(own) * 2 * QUARTER, 2 * QUARTER), 2 * QUARTER)

    (packed,) = call(
        lambda *r: pack_body(rows, *r), "pack", [signal, mel_frames],
        [((DILATION + 8, RESID), f32)], specs=[HBM, HBM],
        scratch=[pltpu.VMEM((slot_count, MELS), f32), pltpu.SemaphoreType.DMA((2,))],
    )
    halo = lax.ppermute(packed, axes, [(i, i + 1) for i in range(count - 1)])

    wide, fine = (bf16, wide8, wide8), (bf16, fine8, fine8)
    half = [((HALF, RESID), t) for t in wide]
    half_gate = [((HALF, RESID), t) for t in fine]
    half32 = ((HALF, HALF), f32)
    square = [((GATE, GATE), t) for t in wide]
    pick = ((HALF, 128), bf16)
    small_scratch = [pltpu.VMEM((128, GATE), bf16), pltpu.VMEM((16, 128), f32)]
    out = call(
        lambda *r: late_body(rows, *r), "late_gates",
        [signal, conv_weight, cond_weight, mel_frames, slots, starts, bias],
        [*half, *half, *half, *square, pick, *half_gate, half32, half32], scratch=small_scratch,
    )
    x0, x1, d1, w = (out[i : i + 3] for i in (0, 3, 6, 9))
    sel1, g1, ca1, cb1 = out[12], out[13:16], out[16], out[17]
    out = call(
        lambda *r: early_body(rows, *r), "early_gates",
        [halo, signal, *x0, *w, cond_weight, mel_frames, slots, starts, bias,
         resid_cotan, skip_cotan, proj_weight],
        [*half, pick, *half_gate, half32, half32, *(((GATE, GATE), t) for t in fine),
         *(((HALF, GATE), t) for t in fine), ((8, GATE), f32)],
        scratch=small_scratch,
    )
    d0, sel0, g0, ca0, cb0 = out[0:3], out[3], out[4:7], out[7], out[8]
    u, p, usum = out[9:12], out[12:15], out[15]

    tiles = ((2 * QUARTER, 8, 128), f32)
    few = 24
    while (QUARTER + few) % max(1, count // 4):
        few += 8
    quarter = QUARTER + few
    wide_tiles = ((2 * quarter, 8, 128), f32)
    state = {}
    sums = {}

    def grad_half(own, scale, stride=None):
        def body(*refs):
            weight_grad(refs[:6], half_cols(own), refs[6:9], refs[9], scale, stride)

        return body

    def proj_grad(own):
        body = grad_half(own, GATED_SCALE * UP_SCALE)
        (out,) = call(body, f"proj_grad{own:d}", [*g0, *g1, *u], [tiles])
        return out

    def tap0_grad(own):
        body = grad_half(own, SIGNAL_SCALE * GRAD_SCALE)
        (out,) = call(body, f"tap0_grad{own:d}", [*d0, *d1, *state["gp"]], [tiles])
        return out

    def tap1_half(own, *refs):
        both, out = refs[9:]
        grad_half(own, SIGNAL_SCALE * GRAD_SCALE, quarter)(*refs[:9], out)
        for q in range(2):
            out[pl.ds(q * quarter + QUARTER, few)] = both[core_half(own) * 2 + q]

    def tap1_first(*refs):
        x, gp, (sel0, sel1, usum, mel, halo) = refs[:6], refs[6:9], refs[9:14]
        out, both, frame_grad, frames = refs[14:]
        sel = jnp.concatenate([sel0[:, 0:16], sel1[:, 0:16]], 0)
        found = dot(sel, gp[0][...], TN)
        found += dot(sel.astype(wide8), gp[2][...], TN) * (1.0 / (LOW * GRAD_SCALE))
        frame_grad[...] = found
        frames[...] = jnp.zeros((16, 128), f32)
        frames[:slot_count, :MELS] = halo[DILATION : DILATION + slot_count, :MELS]
        frames[slot_count : 2 * slot_count, :MELS] = mel[...]
        cond_grad = exact(frames[:, :MELS], found, TN)
        both[...] = jnp.zeros((4, few, 8, 128), f32)
        for q in range(4):
            part = cond_grad[24 * q : min(24 * q + 24, MELS), :]
            put_tiles(both.at[q], part, 0)
        sums = jnp.sum(usum[...], 0, keepdims=True)
        for i in range(8):
            lane = slice(128 * i, 128 * i + 128)
            both[3, 8, i : i + 1, :] = found[15:16, lane]
            both[3, 9, i : i + 1, :] = sums[:, lane]
        tap1_half(False, *x, *gp, both, out)

    def tap1_grad(own):
        ins = [*x0, *x1, *state["gp"]]
        if own:
            (out,) = call(
                lambda *r: tap1_half(True, *r), "tap1_grad1", [*ins, state["few_grad"]], [wide_tiles]
            )
            return out
        out, state["few_grad"], state["frame_grad"] = call(
            tap1_first, "tap1_grad0", [*ins, sel0, sel1, usum, mel_frames, halo],
            [wide_tiles, ((4, few, 8, 128), f32), ((16, GATE), f32)],
            scratch=[pltpu.VMEM((16, 128), f32)],
        )
        return out

    def gate_grad():
        def body(*refs):
            u, p, (ca0, ca1, cb0, cb1), gp = refs[:3], refs[3:6], refs[6:10], refs[10:]
            right = [x[...] for x in p]
            for r in range(0, rows, BLOCK):
                span = slice(r, r + BLOCK)
                grad = product([x[span, :] for x in u], right, NT, UP_SCALE * PROJ_SCALE)
                ca, cb = (ca0, cb0) if r < HALF else (ca1, cb1)
                inner = slice(r % HALF, r % HALF + BLOCK)
                put(gp, (span, slice(0, HALF)), grad * ca[inner, :], GRAD_SCALE)
                put(gp, (span, slice(HALF, GATE)), grad * cb[inner, :], GRAD_SCALE)

        state["gp"] = call(body, "gate_grad", [*u, *p, ca0, ca1, cb0, cb1], square)

    grads = {"P": ("proj", proj_grad), "0": ("tap0", tap0_grad), "1": ("tap1", tap1_grad)}

    def first_half(key):
        name, grad = grads[key]
        whole = WHOLE["P01".index(key)]
        sums[key] = Sum(order, Pairs(name), name, grad(False), whole)

    def second_half(key):
        sums[key].rest = grads[key][1](True)

    def tap_back(gp, w, rows_, tap):
        span = slice(tap * RESID, (tap + 1) * RESID)
        return product(
            [x[rows_, :] for x in gp], [x[span, :] for x in w], NT, GRAD_SCALE * CONV_SCALE
        )

    def back_body(*refs):
        gp, w, (frame_grad, cond, starts, out, own) = refs[:3], refs[3:6], refs[6:]
        usable = columns(usable_row(starts, 0, 128, rows), 128)[0:DILATION]
        out[0:DILATION, :] = tap_back(gp, w, slice(0, DILATION), 0) * usable
        mels = exact(frame_grad[...], cond[...], NT)
        out[DILATION:, :] = jnp.zeros((8, RESID), f32)
        out[DILATION : DILATION + slot_count, :MELS] = mels[:slot_count]
        own[...] = mels[slot_count : 2 * slot_count]
        return []

    def back():
        def done(result):
            state["mel_own"] = result[1]
            state["came"] = lax.ppermute(result[0], axes, [(i, i - 1) for i in range(1, count)])

        return Part(
            "back", [*state["gp"], *w, state["frame_grad"], cond_weight, starts],
            [((DILATION + 8, RESID), f32), ((slot_count, MELS), f32)], back_body, done, to_hbm=False,
        )

    def mix(r):
        def start(*refs):
            g, p, (bias, signal) = refs[:3], refs[3:6], refs[6:8]
            outs, (held, sem) = refs[8:10], refs[10:]
            copies = []
            for s in range(0, HALF, BLOCK):
                inner = slice(s, s + BLOCK)
                span = slice(r + s, r + s + BLOCK)
                left = [x[inner, :] for x in g]
                for k, c in enumerate((0, RESID)):
                    w = slice(c, c + RESID)
                    first = 8 + c // 128
                    row = jnp.concatenate([bias[i : i + 1, :] for i in range(first, first + 4)], 1)
                    mixed = product(left, [x[:, w] for x in p], NN, GATED_SCALE * PROJ_SCALE) + row
                    held[k, inner, :] = mixed + signal[span, :] if k == 0 else mixed
                    copies.append(
                        pltpu.make_async_copy(
                            held.at[k, pl.ds(s, BLOCK)],
                            outs[k].at[pl.ds(r + s, BLOCK)],
                            sem.at[len(copies)],
                        )
                    )
                    copies[-1].start()
            return copies

        return Part(
            "mix", [*(g0 if r < HALF else g1), *p, bias, signal], [((rows, RESID), f32)] * 2,
            start, lambda result: state.update(mixed=result), old=state.get("mixed", ()),
            scratch=[pltpu.VMEM((2, HALF, RESID), f32), pltpu.SemaphoreType.DMA((4,))],
        )

    def signal_grad(r):
        last = r + HALF == rows

        def start(*refs):
            gp, w, (starts, resid_cotan) = refs[:3], refs[3:6], refs[6:8]
            held, mels, sem = refs[-3:]
            copies = []
            if last:
                came, own, out, mel_grad = refs[8:-3]
                mels[...] = own[...] + came[DILATION : DILATION + slot_count, :MELS]
                copies.append(pltpu.make_async_copy(mels, mel_grad, sem.at[2]))
                copies[0].start()
            else:
                out = refs[8]
            usable = columns(usable_row(starts, 0, rows, rows), rows)
            for s in range(r, r + HALF, BLOCK):
                span = slice(s, s + BLOCK)
                ahead = slice(s + DILATION, min(s + DILATION + BLOCK, rows))
                inner = slice(s - r, s - r + BLOCK)
                later = tap_back(gp, w, ahead, 0) * usable[ahead]
                held[inner, :] = tap_back(gp, w, span, 1) + resid_cotan[span, :]
                held[s - r : s - r + later.shape[0], :] += later
                if s + BLOCK == rows:
                    held[HALF - DILATION :, :] += came[0:DILATION, :]
                copies.append(
                    pltpu.make_async_copy(
                        held.at[pl.ds(s - r, BLOCK)], out.at[pl.ds(s, BLOCK)], sem.at[(s - r) // BLOCK]
                    )
                )
                copies[-1].start()
            return copies

        ins = [*state["gp"], *w, starts, resid_cotan]
        outs = [((rows, RESID), f32)]
        if last:
            ins += [state["came"], state["mel_own"]]
            outs += [((slot_count, MELS), f32)]
        return Part(
            "sg", ins, outs, start, lambda result: state.update(signal_grad=result),
            old=state.get("signal_grad", ()),
            scratch=[pltpu.VMEM((HALF, RESID), f32), pltpu.VMEM((slot_count, MELS), f32),
                     pltpu.SemaphoreType.DMA((3,))],
        )

    root = math.sqrt(rows * count)
    conv_rate = step_scale / (math.sqrt(2 * RESID) * 1.5 * root)
    cond_rate = step_scale / (math.sqrt(MELS) * 1.5 * root)
    proj_rate = step_scale / (math.sqrt(GATE // 16) * 0.3 * root)
    biases_rate = step_scale * 0.3 / (1.2 * root)

    def step_tile(g, w, m, a, rate):
        m = momentum_rate * m + g
        w = w - rate * (g + momentum_rate * m)
        return w, m, ema_decay * a + (1.0 - ema_decay) * w

    conv = (conv_weight, conv_moment, conv_average)
    matrices = {
        "proj": ((proj_weight, proj_moment, proj_average), proj_rate),
        "conv": (conv, conv_rate),
    }
    kinds = (f32, f32, f32, bf16)
    few_args = (cond_weight, cond_moment, cond_average, bias,
                biases_moment.reshape(16, 128), biases_average.reshape(16, 128))
    few_shapes = [((MELS, GATE), t) for t in kinds] + [((16, 128), t) for t in kinds]

    def update_few(pieces, ins, outs, held, grads, sem):
        for k, piece in enumerate(pieces):
            first = sums["1"].pairs.quarter(k) * 24
            grads[pl.ds(first, 24)] = piece[QUARTER : QUARTER + 24]
        for r in range(0, MELS, 16):
            span = slice(r, r + 16)
            for c in range(0, GATE, 128):
                w = slice(c, c + 128)
                tile = r + c // 128
                g = jnp.concatenate([grads[tile], grads[tile + 8]], 0)
                new = step_tile(g, *(x[span, w] for x in ins[:3]), cond_rate)
                for ref, value in zip(held, new):
                    ref[span, w] = value
                held[3][span, w] = new[0].astype(bf16)
        grad = jnp.concatenate([grads[MELS], grads[MELS + 1]], 0)
        new = step_tile(grad, *(x[...] for x in ins[3:]), biases_rate)
        for ref, value in zip(held[4:], new):
            ref[...] = value
        held[7][...] = new[0].astype(bf16)
        copies = [
            pltpu.make_async_copy(a, b, sem.at[i]) for i, (a, b) in enumerate(zip(held, outs))
        ]
        for copy in copies:
            copy.start()
        return copies

    def update(key, items):
        trio, rate = matrices[key]
        n = len(items)

        def start(*refs):
            gs, trio_refs, outs = refs[:n], refs[n : n + 3], refs[n + 3 : n + 7]
            held, sem = refs[n + 7 : n + 11], refs[n + 11]
            copies = []
            for i, (total, k, lead) in enumerate(items):
                first = pl.multiple_of(total.pairs.quarter(k) * QUARTER, QUARTER)
                parts = [x if lead is None else x.at[lead] for x in (*trio_refs, *outs)]
                for r in range(0, QUARTER, 16):
                    span = slice(i * QUARTER + r, i * QUARTER + r + 16)
                    there = pl.ds(first + r, 16)
                    for c in range(0, GATE, 128):
                        w = slice(c, c + 128)
                        tile = r + c // 128
                        g = jnp.concatenate([gs[i][tile], gs[i][tile + 8]], 0)
                        new = step_tile(g, *(x[there, w] for x in parts[:3]), rate)
                        for ref, value in zip(held, new):
                            ref[span, w] = value
                        held[3][span, w] = new[0].astype(bf16)
                for o in range(4):
                    copies.append(
                        pltpu.make_async_copy(
                            held[o].at[pl.ds(i * QUARTER, QUARTER)],
                            parts[3 + o].at[pl.ds(first, QUARTER)],
                            sem.at[i * 4 + o],
                        )
                    )
                    copies[-1].start()
            return copies

        return Part(
            f"u{n}", [total.pieces[k] for total, k, _ in items] + [*trio],
            [(trio[0].shape, t) for t in kinds], start,
            lambda result: state.update({key: result}), old=state.get(key, ()),
            scratch=[pltpu.VMEM((n * QUARTER, GATE), t) for t in kinds]
            + [pltpu.SemaphoreType.DMA((4 * n,))],
        )

    def few_update():
        def start(*refs):
            return update_few(refs[:4], refs[4:10], refs[10:18], refs[18:26], refs[26], refs[27])

        return Part(
            "few", [*sums["1"].pieces, *few_args], few_shapes, start,
            lambda result: state.update(few=result),
            scratch=[pltpu.VMEM(*x) for x in few_shapes]
            + [pltpu.VMEM((96, 8, 128), f32), pltpu.SemaphoreType.DMA((8,))],
        )

    def spread(key):
        total = sums[key]
        while not total.done:
            total.advance()
        total.pieces = [total.piece, total.pairs.swap(total.piece, 0), total.pairs.swap(total.piece, 1)]

    def relay(key):
        total = sums[key]
        total.pieces.append(total.pairs.swap(total.pieces[2], 0))

    owners = {"P": ("proj", None), "0": ("conv", 0), "1": ("conv", 1)}
    fill = {"back": back}
    for i in range(2):
        fill[f"mix{i}"] = lambda i=i: mix(i * HALF)
        fill[f"sg{i}"] = lambda i=i: signal_grad(i * HALF)

    def updates(word):
        named = {}
        for letter in word[1:]:
            if letter in owners:
                key, lead = owners[letter]
                total = sums[letter]
            elif letter in "abcd":
                named.setdefault(key, []).append((total, "abcd".index(letter), lead))
        return [update(key, items) for key, items in named.items()] + (
            [few_update()] if "f" in word else []
        )

    for word in SCRIPT.split():
        if word in owners:
            sums[word].advance()
        elif word == "gg":
            gate_grad()
        elif len(word) == 2 and word[0] in "jksr":
            {"j": first_half, "k": second_half, "s": spread, "r": relay}[word[0]](word[1])
        else:
            work = []
            for item in word.split("+"):
                work += updates(item) if item[0] == "=" else [fill[item]()]
            run_parts(order, work)
    proj_new, conv_new = state["proj"], state["conv"]
    cond_new, bias_new = state["few"][:4], [x.reshape(-1) for x in state["few"][4:]]
    result = [*state["mixed"], *state["signal_grad"]]
    for k in range(4):
        result += [conv_new[k], cond_new[k], proj_new[k], bias_new[k]]
    return tuple(result)


WHOLE = (2, 1, 1)
SCRIPT = """
jP gg kP P j0 k0 j1 k1 P 0 sg0 P 1 back 0 mix0 P 1 mix1 0 1 P 0 1 0 P 1 0 sP rP sg1 1 0 s0 1 s1 =Pb r0 =0abPacd
r1 =1a =0cd1bc =1df
"""


def shards(*args):
    return solve(Pairs("proj"), args)


def solution(mesh):
    rows = P(("blk", "seq"), None)
    in_specs = (rows, P(("blk", "seq")), P(("blk", "seq")), rows, rows, rows) + (P(),) * 12
    out_specs = (rows,) * 4 + (P(),) * 16
    return jax.shard_map(shards, mesh=mesh, in_specs=in_specs, out_specs=out_specs, check_vma=False)
```

```python
import math

import jax
import jax.numpy as jnp
from jax import lax
from jax.experimental import pallas as pl
from jax.experimental.pallas import tpu as pltpu
from jax.sharding import PartitionSpec as P

RESID = 512
GATE = 1024
MELS = 80
DILATION = 64
HALF = 512

f32 = jnp.float32
bf16 = jnp.bfloat16
momentum_rate = 0.9
ema_decay = 0.5
step_scale = 0.15
axes = ("blk", "seq")

VMEM = pl.BlockSpec(memory_space=pltpu.VMEM)
HBM = pl.BlockSpec(memory_space=pltpu.HBM)
ANY = pl.BlockSpec(memory_space=pl.ANY)
MIB = 1 << 20


TOKEN = ((8, 128), f32)

RATE = 2.9e9
TIMES = {
    "pack": 1, "late_gates": 4, "early_gates": 4.4, "gate_grad": 3.4, "proj_grad": 1.4, "tap0_grad": 1.4,
    "tap1_grad0": 2, "tap1_grad1": 1.4,
}
WORK = {"do": 0.7, "mix": 1.5, "sg": 2.8, "back": 0.5, "few": 0.8, "u1": 0.7, "u2": 1.3, "u3": 1.9, "u4": 2.5}
FOLD = 0.03


def expected(name):
    if name.startswith("do_"):
        return sum(WORK.get(word, 3) for word in name.split("_"))
    for key in sorted(TIMES, key=len, reverse=True):
        if key in name:
            return TIMES[key]
    return FOLD


class Order:
    def __init__(self):
        self.last = None

    def call(
        self, body, name, ins, outs, specs=None, out_specs=None, scratch=(), limit=16, aliases=None
    ):
        specs = list(specs) if specs else [VMEM] * len(ins)
        ins = [
            pltpu.with_memory_space_constraint(x, pltpu.HBM) if s is HBM else x
            for x, s in zip(ins, specs)
        ]
        out_specs = list(out_specs) if out_specs else [VMEM] * len(outs)
        after = [] if self.last is None else [self.last]
        n_in, n_after, n_out = len(ins), len(after), len(outs)

        def run(*refs):
            outs = refs[n_in + n_after : n_in + n_after + n_out]
            token = refs[n_in + n_after + n_out]
            token[...] = jnp.zeros(token.shape, f32)
            body(*refs[:n_in], *outs, *refs[n_in + n_after + n_out + 1 :])

        kinds = {id(VMEM): pltpu.VMEM, id(HBM): pltpu.HBM}
        *result, self.last = pl.pallas_call(
            run,
            out_shape=[kinds[id(s)](*o) for o, s in zip(outs, out_specs)] + [pltpu.VMEM(*TOKEN)],
            in_specs=specs + [VMEM] * n_after,
            out_specs=out_specs + [VMEM],
            scratch_shapes=list(scratch),
            input_output_aliases=aliases or {},
            compiler_params=pltpu.CompilerParams(vmem_limit_bytes=limit * MIB),
            cost_estimate=pl.CostEstimate(
                flops=int(RATE * expected(name)), bytes_accessed=1, transcendentals=0
            ),
            name=name,
        )(*ins, *after)
        return result


wide8 = jnp.float8_e5m2
fine8 = jnp.float8_e4m3fn
SIGNAL_SCALE, CONV_SCALE, GRAD_SCALE = 2.0**12, 2.0**18, 2.0**3
UP_SCALE, PROJ_SCALE, GATED_SCALE = 2.0**6, 2.0**9, 2.0**8
LOW = 256.0


def split(x):
    high = x.astype(bf16)
    return high, (x - high.astype(f32)).astype(bf16)


class Part:
    def __init__(self, name, ins, outs, start, done, old=(), scratch=(), to_hbm=True):
        self.name, self.ins, self.outs, self.start, self.done = name, list(ins), list(outs), start, done
        self.old, self.scratch, self.to_hbm = list(old), list(scratch), to_hbm


def run_parts(order, parts):
    ins, specs, outs, out_specs, scratch, aliases = [], [], [], [], [], {}
    for part in parts:
        for i in range(len(part.old)):
            aliases[len(ins) + len(part.ins) + i] = len(outs) + i
        ins += part.ins + part.old
        specs += [VMEM] * len(part.ins) + [HBM] * len(part.old)
        outs += part.outs
        out_specs += [HBM if part.to_hbm else VMEM] * len(part.outs)
        scratch += part.scratch
    n_in, n_out = len(ins), len(outs)

    def body(*refs):
        ins, outs, scratch = list(refs[:n_in]), list(refs[n_in : n_in + n_out]), list(refs[n_in + n_out :])
        copies = []
        for part in parts:
            mine = [ins.pop(0) for _ in part.ins]
            del ins[: len(part.old)]
            mine += [outs.pop(0) for _ in part.outs]
            mine += [scratch.pop(0) for _ in part.scratch]
            copies += part.start(*mine)
        for copy in copies:
            copy.wait()

    name = "_".join(["do"] + [part.name for part in parts])
    result = order.call(
        body, name, ins, outs, specs=specs, out_specs=out_specs, scratch=scratch, aliases=aliases, limit=20
    )
    for part in parts:
        part.done([result.pop(0) for _ in part.outs])


def put(refs, where, x, scale):
    high = x.astype(bf16)
    refs[0][where] = high
    refs[1][where] = (high * bf16(scale)).astype(refs[1].dtype)
    refs[2][where] = ((x - high.astype(f32)) * (scale * LOW)).astype(refs[2].dtype)


def dot(left, right, over):
    return lax.dot_general(left, right, (over, ((), ())), preferred_element_type=f32)


def product(left, right, over, scale):
    axis = [o[0] for o in over]
    low = jnp.concatenate([left[2], left[1]], axis[0])
    high = jnp.concatenate([right[1], right[2]], axis[1])
    return dot(left[0], right[0], over) + dot(low, high, over) * (1.0 / (LOW * scale))


def exact(left, right, over):
    return lax.dot_general(
        left, right, (over, ((), ())), preferred_element_type=f32, precision=lax.Precision.HIGHEST
    )


NN = ((1,), (0,))
NT = ((1,), (1,))
TN = ((0,), (0,))


ORDERS = {
    "proj": ((2, 1, 3, 4), (1, 2, 4, 3)),
    "tap0": ((2, 3, 1, 4), (1, 4, 2, 3)),
    "tap1": ((2, 1, 3, 4), (1, 2, 4, 3)),
}
LARGE = ((6, 0, 3, 7, 1, 4, 5), (0, 6, 3, 1, 7, 4, 5))


def plan(blk, seq, name):
    if (blk, seq) == (8, 4):
        return 0, ORDERS[name]
    if (blk, seq) == (64, 4):
        return 2, LARGE
    rest = tuple(range(1, (blk * seq).bit_length() - 1))
    return 0, (rest, rest)


class Pairs:
    def __init__(self, name):
        blk, seq = lax.axis_size("blk"), lax.axis_size("seq")
        self.count = blk * seq
        self.core_bit, (first, second) = plan(blk, seq, name)
        self.places = [(self.core_bit, self.core_bit), *zip(first, second)]
        self.steps = len(self.places)
        self.pairs = [
            [(i, i ^ (1 << p[(i >> self.core_bit) & 1])) for i in range(self.count)]
            for p in self.places
        ]

    def bit(self, step, sibling=False):
        me = lax.axis_index(axes)
        core = (me >> self.core_bit) & 1
        if sibling:
            core = 1 - core
        if step == 0:
            return core
        a, b = self.places[step]
        return jnp.where(core == 0, (me >> a) & 1, (me >> b) & 1)

    def quarter(self, k):
        core, bit = self.bit(0), self.bit(1, k % 2 == 1)
        return (1 - core if k % 2 else core) * 2 + (1 - bit if k >= 2 else bit)

    def swap(self, x, step):
        return lax.ppermute(x, axes, self.pairs[step])


class Sum:
    def __init__(self, order, pairs, name, send, whole=1):
        self.order, self.pairs, self.name = order, pairs, name
        self.parted = pairs.steps - whole
        self.step, self.back = 0, False
        self.got = pairs.swap(send, 0)
        self.done = False

    def advance(self):
        if self.done:
            return
        pairs, step = self.pairs, self.step
        label = f"{self.name}_{'join' if self.back else 'fold'}{step}"
        if self.back:
            size = self.piece.shape[0]

            def body(mine, got, out):
                bit = pairs.bit(step)
                out[pl.ds(bit * size, size)] = mine[...]
                out[pl.ds((1 - bit) * size, size)] = got[...]

            (self.piece,) = self.order.call(
                body, label, [self.piece, self.got], [((2 * size, 8, 128), f32)]
            )
            self.step -= 1
        elif step + 1 < self.parted:
            half = self.rest.shape[0] // 2

            def body(keep, got, send, rest):
                bit = pairs.bit(step + 1)
                here, there = pl.ds(bit * half, half), pl.ds((1 - bit) * half, half)
                send[...] = keep[there] + got[there]
                rest[...] = keep[here] + got[here]

            shape = ((half, 8, 128), f32)
            send, self.rest = self.order.call(body, label, [self.rest, self.got], [shape, shape])
            self.step += 1
            self.got = pairs.swap(send, self.step)
            return
        else:
            mine = self.rest if step < self.parted else self.piece

            def body(mine, got, out):
                out[...] = mine[...] + got[...]

            (self.piece,) = self.order.call(body, label, [mine, self.got], [(mine.shape, f32)])
            self.step += 1
            if self.step == pairs.steps:
                self.back, self.step = True, self.parted - 1
        if self.back and self.step == 1:
            self.done = True
            return
        self.got = pairs.swap(self.piece, self.step)


def pack_body(rows, signal, mel, out, frames, sem):
    copy = pltpu.make_async_copy(
        signal.at[pl.ds(rows - DILATION, DILATION)], out.at[pl.ds(0, DILATION)], sem.at[0]
    )
    other = pltpu.make_async_copy(mel, frames, sem.at[1])
    copy.start()
    other.start()
    out[DILATION:, :] = jnp.zeros((8, RESID), f32)
    other.wait()
    out[DILATION : DILATION + mel.shape[0], :MELS] = frames[...]
    copy.wait()


def columns(row, rows):
    return jnp.transpose(jnp.broadcast_to(row, (8, rows)))[:, :1]


def picks(slots, part, slot_count, sel):
    me = lax.axis_index(axes)
    local = (slots[:, part * HALF : (part + 1) * HALF] - (me - 1) * slot_count).astype(f32)
    local = columns(local, HALF).astype(jnp.int32)
    lane = lax.broadcasted_iota(jnp.int32, (HALF, 128), 1)
    hot = (lane == local) | (lane == local + 16) | (lane == 15)
    sel[...] = jnp.where(hot, 1.0, 0.0).astype(bf16)


def usable_row(starts, first, count, row_count):
    time = lax.axis_index(axes) * row_count + first + lax.broadcasted_iota(jnp.int32, (1, count), 1)
    return jnp.where(time - DILATION >= starts[:, first : first + count], 1.0, 0.0)


def frame_terms(mel, prior, cond, bias, table, frames):
    slot_count = mel.shape[0]
    frames[...] = jnp.zeros((16, 128), f32)
    frames[slot_count : 2 * slot_count, :MELS] = mel[...]
    if prior is not None:
        frames[:slot_count, :MELS] = prior
    row = jnp.concatenate([bias[i : i + 1, :] for i in range(8)], 1)
    terms = exact(frames[:, :MELS], cond[...], NN) + row
    keep = lax.broadcasted_iota(jnp.int32, (16, GATE), 0) < 2 * slot_count
    high, low = split(jnp.where(keep, terms, 0.0))
    table[...] = jnp.zeros((128, GATE), bf16)
    table[0:16, :] = high
    table[16:32, :] = low


def gates(tanh_in, sigm_in, cols, g, ca, cb):
    th = jnp.tanh(tanh_in)
    sg = 0.5 * jnp.tanh(0.5 * sigm_in) + 0.5
    gated = th * sg
    put(g, (slice(None), cols), gated, GATED_SCALE)
    ca[:, cols] = sg * (1.0 - th * th)
    cb[:, cols] = gated * (1.0 - sg)


def preact_block(d, x, sel, w, table, cols):
    main = dot(
        jnp.concatenate([d[0][...], x[0][...], sel[...]], 1),
        jnp.concatenate([w[0][:, cols], table[:, cols]], 0),
        NN,
    )
    low = dot(
        jnp.concatenate([d[2][...], x[2][...], d[1][...], x[1][...]], 1),
        jnp.concatenate([w[1][:, cols], w[2][:, cols]], 0),
        NN,
    )
    return main + low * (1.0 / (LOW * SIGNAL_SCALE * CONV_SCALE))


BLOCK = 256


def late_body(rows, *refs):
    signal, conv, cond, mel, slots, starts, bias = refs[:7]
    x0, x1, d, w = (refs[i : i + 3] for i in (7, 10, 13, 16))
    sel, g, ca, cb, table, frames = refs[19], refs[20:23], *refs[23:]
    first = HALF - DILATION
    picks(slots, 1, mel.shape[0], sel)
    frame_terms(mel, None, cond, bias, table, frames)
    usable = columns(usable_row(starts, HALF, HALF, rows), HALF)
    put(x1, slice(None), signal[HALF:, :], SIGNAL_SCALE)
    put(d, slice(None), signal[first : first + HALF, :] * usable, SIGNAL_SCALE)
    for j in range(HALF // BLOCK):
        blocks = [slice(c + j * BLOCK, c + (j + 1) * BLOCK) for c in (0, HALF)]
        products = []
        for cols in blocks:
            for tap in range(2):
                span = slice(tap * RESID, (tap + 1) * RESID)
                put(w, (span, cols), conv[tap, :, cols], CONV_SCALE)
            products.append(preact_block(d, x1, sel, w, table, cols))
        gates(*products, blocks[0], g, ca, cb)
    put(x0, slice(None), signal[0:HALF, :], SIGNAL_SCALE)


def early_body(rows, *refs):
    halo, signal = refs[:2]
    x, w = refs[2:5], refs[5:8]
    cond, mel, slots, starts, bias, resid_cotan, skip_cotan, proj = refs[8:16]
    d, sel, g, ca, cb = refs[16:19], refs[19], refs[20:23], refs[23], refs[24]
    u, p, usum, table, frames = refs[25:28], refs[28:31], *refs[31:]
    picks(slots, 0, mel.shape[0], sel)
    frame_terms(mel, halo[DILATION : DILATION + mel.shape[0], :MELS], cond, bias, table, frames)
    usable = columns(usable_row(starts, 0, HALF, rows), HALF)
    put(d, slice(0, DILATION), halo[0:DILATION, :] * usable[0:DILATION], SIGNAL_SCALE)
    rest = HALF - DILATION
    put(d, slice(DILATION, None), signal[0:rest, :] * usable[DILATION:], SIGNAL_SCALE)
    totals = [jnp.zeros((8, RESID), f32), jnp.zeros((8, RESID), f32)]

    def part_cotangents(first, count):
        for r in range(first, first + count, 32):
            for k, part in enumerate((resid_cotan, skip_cotan)):
                value = part[r : r + 32, :]
                put(u, (slice(r, r + 32), slice(k * RESID, (k + 1) * RESID)), value, UP_SCALE)
                totals[k] = totals[k] + jnp.sum(value.reshape(4, 8, RESID), 0)

    for r in range(0, HALF, 32):
        put(p, slice(r, r + 32), proj[r : r + 32, :], PROJ_SCALE)
    for j in range(HALF // BLOCK):
        tc, sc = (slice(c + j * BLOCK, c + (j + 1) * BLOCK) for c in (0, HALF))
        part_cotangents(j * rows // 2, rows // 4)
        tanh_in = preact_block(d, x, sel, w, table, tc)
        part_cotangents(j * rows // 2 + rows // 4, rows // 4)
        sigm_in = preact_block(d, x, sel, w, table, sc)
        gates(tanh_in, sigm_in, tc, g, ca, cb)
    usum[...] = jnp.concatenate(totals, 1)


def put_tiles(out, value, col0, stride=None):
    height, width = value.shape
    for r in range(height // 8):
        base = r * 8 if stride is None else (r * 8 // QUARTER) * stride + (r * 8) % QUARTER
        for c in range(width // 128):
            out[base + col0 // 128 + c] = value[8 * r : 8 * r + 8, 128 * c : 128 * c + 128]


WIDE = 512


def weight_grad(left, cols, right, out, scale, stride=None):
    left = [jnp.concatenate([a[:, cols], b[:, cols]], 0) for a, b in zip(left[:3], left[3:])]
    for c in range(0, GATE, WIDE):
        wide = [r[:, c : c + WIDE] for r in right]
        put_tiles(out, product(left, wide, TN, scale), c, stride)


QUARTER = 128


def solve(pairs, args):
    (
        signal, item_start, frame_slot, mel_frames, resid_cotan, skip_cotan,
        conv_weight, cond_weight, proj_weight, biases,
        conv_moment, cond_moment, proj_moment, biases_moment,
        conv_average, cond_average, proj_average, biases_average,
    ) = args
    rows = signal.shape[0]
    slot_count = mel_frames.shape[0]
    slots = frame_slot.reshape(1, rows)
    starts = item_start.reshape(1, rows)
    bias = biases.reshape(16, 128)
    count = pairs.count
    order = Order()
    call = order.call

    def core_half(own):
        bit = pairs.bit(0)
        return bit if own else 1 - bit

    def half_cols(own):
        return pl.ds(pl.multiple_of(core_half(own) * 2 * QUARTER, 2 * QUARTER), 2 * QUARTER)

    (packed,) = call(
        lambda *r: pack_body(rows, *r), "pack", [signal, mel_frames],
        [((DILATION + 8, RESID), f32)], specs=[HBM, HBM],
        scratch=[pltpu.VMEM((slot_count, MELS), f32), pltpu.SemaphoreType.DMA((2,))],
    )
    halo = lax.ppermute(packed, axes, [(i, i + 1) for i in range(count - 1)])

    wide, fine = (bf16, wide8, wide8), (bf16, fine8, fine8)
    half = [((HALF, RESID), t) for t in wide]
    half_gate = [((HALF, RESID), t) for t in fine]
    half32 = ((HALF, HALF), f32)
    square = [((GATE, GATE), t) for t in wide]
    pick = ((HALF, 128), bf16)
    small_scratch = [pltpu.VMEM((128, GATE), bf16), pltpu.VMEM((16, 128), f32)]
    out = call(
        lambda *r: late_body(rows, *r), "late_gates",
        [signal, conv_weight, cond_weight, mel_frames, slots, starts, bias],
        [*half, *half, *half, *square, pick, *half_gate, half32, half32], scratch=small_scratch,
    )
    x0, x1, d1, w = (out[i : i + 3] for i in (0, 3, 6, 9))
    sel1, g1, ca1, cb1 = out[12], out[13:16], out[16], out[17]
    out = call(
        lambda *r: early_body(rows, *r), "early_gates",
        [halo, signal, *x0, *w, cond_weight, mel_frames, slots, starts, bias,
         resid_cotan, skip_cotan, proj_weight],
        [*half, pick, *half_gate, half32, half32, *(((GATE, GATE), t) for t in fine),
         *(((HALF, GATE), t) for t in fine), ((8, GATE), f32)],
        scratch=small_scratch,
    )
    d0, sel0, g0, ca0, cb0 = out[0:3], out[3], out[4:7], out[7], out[8]
    u, p, usum = out[9:12], out[12:15], out[15]

    tiles = ((2 * QUARTER, 8, 128), f32)
    few = 24
    while (QUARTER + few) % max(1, count // 4):
        few += 8
    quarter = QUARTER + few
    wide_tiles = ((2 * quarter, 8, 128), f32)
    state = {}
    sums = {}

    def grad_half(own, scale, stride=None):
        def body(*refs):
            weight_grad(refs[:6], half_cols(own), refs[6:9], refs[9], scale, stride)

        return body

    def proj_grad(own):
        body = grad_half(own, GATED_SCALE * UP_SCALE)
        (out,) = call(body, f"proj_grad{own:d}", [*g0, *g1, *u], [tiles])
        return out

    def tap0_grad(own):
        body = grad_half(own, SIGNAL_SCALE * GRAD_SCALE)
        (out,) = call(body, f"tap0_grad{own:d}", [*d0, *d1, *state["gp"]], [tiles])
        return out

    def tap1_half(own, *refs):
        both, out = refs[9:]
        grad_half(own, SIGNAL_SCALE * GRAD_SCALE, quarter)(*refs[:9], out)
        for q in range(2):
            out[pl.ds(q * quarter + QUARTER, few)] = both[core_half(own) * 2 + q]

    def tap1_first(*refs):
        x, gp, (sel0, sel1, usum, mel, halo) = refs[:6], refs[6:9], refs[9:14]
        out, both, frame_grad, frames = refs[14:]
        sel = jnp.concatenate([sel0[:, 0:16], sel1[:, 0:16]], 0)
        found = dot(sel, gp[0][...], TN)
        found += dot(sel.astype(wide8), gp[2][...], TN) * (1.0 / (LOW * GRAD_SCALE))
        frame_grad[...] = found
        frames[...] = jnp.zeros((16, 128), f32)
        frames[:slot_count, :MELS] = halo[DILATION : DILATION + slot_count, :MELS]
        frames[slot_count : 2 * slot_count, :MELS] = mel[...]
        cond_grad = exact(frames[:, :MELS], found, TN)
        both[...] = jnp.zeros((4, few, 8, 128), f32)
        for q in range(4):
            part = cond_grad[24 * q : min(24 * q + 24, MELS), :]
            put_tiles(both.at[q], part, 0)
        sums = jnp.sum(usum[...], 0, keepdims=True)
        for i in range(8):
            lane = slice(128 * i, 128 * i + 128)
            both[3, 8, i : i + 1, :] = found[15:16, lane]
            both[3, 9, i : i + 1, :] = sums[:, lane]
        tap1_half(False, *x, *gp, both, out)

    def tap1_grad(own):
        ins = [*x0, *x1, *state["gp"]]
        if own:
            (out,) = call(
                lambda *r: tap1_half(True, *r), "tap1_grad1", [*ins, state["few_grad"]], [wide_tiles]
            )
            return out
        out, state["few_grad"], state["frame_grad"] = call(
            tap1_first, "tap1_grad0", [*ins, sel0, sel1, usum, mel_frames, halo],
            [wide_tiles, ((4, few, 8, 128), f32), ((16, GATE), f32)],
            scratch=[pltpu.VMEM((16, 128), f32)],
        )
        return out

    def gate_grad():
        def body(*refs):
            u, p, (ca0, ca1, cb0, cb1), gp = refs[:3], refs[3:6], refs[6:10], refs[10:]
            right = [x[...] for x in p]
            for r in range(0, rows, BLOCK):
                span = slice(r, r + BLOCK)
                grad = product([x[span, :] for x in u], right, NT, UP_SCALE * PROJ_SCALE)
                ca, cb = (ca0, cb0) if r < HALF else (ca1, cb1)
                inner = slice(r % HALF, r % HALF + BLOCK)
                put(gp, (span, slice(0, HALF)), grad * ca[inner, :], GRAD_SCALE)
                put(gp, (span, slice(HALF, GATE)), grad * cb[inner, :], GRAD_SCALE)

        state["gp"] = call(body, "gate_grad", [*u, *p, ca0, ca1, cb0, cb1], square)

    grads = {"P": ("proj", proj_grad), "0": ("tap0", tap0_grad), "1": ("tap1", tap1_grad)}

    def first_half(key):
        name, grad = grads[key]
        whole = WHOLE["P01".index(key)]
        sums[key] = Sum(order, Pairs(name), name, grad(False), whole)

    def second_half(key):
        sums[key].rest = grads[key][1](True)

    def tap_back(gp, w, rows_, tap):
        span = slice(tap * RESID, (tap + 1) * RESID)
        return product(
            [x[rows_, :] for x in gp], [x[span, :] for x in w], NT, GRAD_SCALE * CONV_SCALE
        )

    def back_body(*refs):
        gp, w, (frame_grad, cond, starts, out, own) = refs[:3], refs[3:6], refs[6:]
        usable = columns(usable_row(starts, 0, 128, rows), 128)[0:DILATION]
        out[0:DILATION, :] = tap_back(gp, w, slice(0, DILATION), 0) * usable
        mels = exact(frame_grad[...], cond[...], NT)
        out[DILATION:, :] = jnp.zeros((8, RESID), f32)
        out[DILATION : DILATION + slot_count, :MELS] = mels[:slot_count]
        own[...] = mels[slot_count : 2 * slot_count]
        return []

    def back():
        def done(result):
            state["mel_own"] = result[1]
            state["came"] = lax.ppermute(result[0], axes, [(i, i - 1) for i in range(1, count)])

        return Part(
            "back", [*state["gp"], *w, state["frame_grad"], cond_weight, starts],
            [((DILATION + 8, RESID), f32), ((slot_count, MELS), f32)], back_body, done, to_hbm=False,
        )

    def mix(r):
        def start(*refs):
            g, p, (bias, signal) = refs[:3], refs[3:6], refs[6:8]
            outs, (held, sem) = refs[8:10], refs[10:]
            copies = []
            for s in range(0, HALF, BLOCK):
                inner = slice(s, s + BLOCK)
                span = slice(r + s, r + s + BLOCK)
                left = [x[inner, :] for x in g]
                for k, c in enumerate((0, RESID)):
                    w = slice(c, c + RESID)
                    first = 8 + c // 128
                    row = jnp.concatenate([bias[i : i + 1, :] for i in range(first, first + 4)], 1)
                    mixed = product(left, [x[:, w] for x in p], NN, GATED_SCALE * PROJ_SCALE) + row
                    held[k, inner, :] = mixed + signal[span, :] if k == 0 else mixed
                    copies.append(
                        pltpu.make_async_copy(
                            held.at[k, pl.ds(s, BLOCK)],
                            outs[k].at[pl.ds(r + s, BLOCK)],
                            sem.at[len(copies)],
                        )
                    )
                    copies[-1].start()
            return copies

        return Part(
            "mix", [*(g0 if r < HALF else g1), *p, bias, signal], [((rows, RESID), f32)] * 2,
            start, lambda result: state.update(mixed=result), old=state.get("mixed", ()),
            scratch=[pltpu.VMEM((2, HALF, RESID), f32), pltpu.SemaphoreType.DMA((4,))],
        )

    def signal_grad(r):
        last = r + HALF == rows

        def start(*refs):
            gp, w, (starts, resid_cotan) = refs[:3], refs[3:6], refs[6:8]
            held, mels, sem = refs[-3:]
            copies = []
            if last:
                came, own, out, mel_grad = refs[8:-3]
                mels[...] = own[...] + came[DILATION : DILATION + slot_count, :MELS]
                copies.append(pltpu.make_async_copy(mels, mel_grad, sem.at[2]))
                copies[0].start()
            else:
                out = refs[8]
            usable = columns(usable_row(starts, 0, rows, rows), rows)
            for s in range(r, r + HALF, BLOCK):
                span = slice(s, s + BLOCK)
                ahead = slice(s + DILATION, min(s + DILATION + BLOCK, rows))
                inner = slice(s - r, s - r + BLOCK)
                later = tap_back(gp, w, ahead, 0) * usable[ahead]
                held[inner, :] = tap_back(gp, w, span, 1) + resid_cotan[span, :]
                held[s - r : s - r + later.shape[0], :] += later
                if s + BLOCK == rows:
                    held[HALF - DILATION :, :] += came[0:DILATION, :]
                copies.append(
                    pltpu.make_async_copy(
                        held.at[pl.ds(s - r, BLOCK)], out.at[pl.ds(s, BLOCK)], sem.at[(s - r) // BLOCK]
                    )
                )
                copies[-1].start()
            return copies

        ins = [*state["gp"], *w, starts, resid_cotan]
        outs = [((rows, RESID), f32)]
        if last:
            ins += [state["came"], state["mel_own"]]
            outs += [((slot_count, MELS), f32)]
        return Part(
            "sg", ins, outs, start, lambda result: state.update(signal_grad=result),
            old=state.get("signal_grad", ()),
            scratch=[pltpu.VMEM((HALF, RESID), f32), pltpu.VMEM((slot_count, MELS), f32),
                     pltpu.SemaphoreType.DMA((3,))],
        )

    root = math.sqrt(rows * count)
    conv_rate = step_scale / (math.sqrt(2 * RESID) * 1.5 * root)
    cond_rate = step_scale / (math.sqrt(MELS) * 1.5 * root)
    proj_rate = step_scale / (math.sqrt(GATE // 16) * 0.3 * root)
    biases_rate = step_scale * 0.3 / (1.2 * root)

    def step_tile(g, w, m, a, rate):
        m = momentum_rate * m + g
        w = w - rate * (g + momentum_rate * m)
        return w, m, ema_decay * a + (1.0 - ema_decay) * w

    conv = (conv_weight, conv_moment, conv_average)
    matrices = {
        "proj": ((proj_weight, proj_moment, proj_average), proj_rate),
        "conv": (conv, conv_rate),
    }
    kinds = (f32, f32, f32, bf16)
    few_args = (cond_weight, cond_moment, cond_average, bias,
                biases_moment.reshape(16, 128), biases_average.reshape(16, 128))
    few_shapes = [((MELS, GATE), t) for t in kinds] + [((16, 128), t) for t in kinds]

    def update_few(pieces, ins, outs, held, grads, sem):
        for k, piece in enumerate(pieces):
            first = sums["1"].pairs.quarter(k) * 24
            grads[pl.ds(first, 24)] = piece[QUARTER : QUARTER + 24]
        for r in range(0, MELS, 16):
            span = slice(r, r + 16)
            for c in range(0, GATE, 128):
                w = slice(c, c + 128)
                tile = r + c // 128
                g = jnp.concatenate([grads[tile], grads[tile + 8]], 0)
                new = step_tile(g, *(x[span, w] for x in ins[:3]), cond_rate)
                for ref, value in zip(held, new):
                    ref[span, w] = value
                held[3][span, w] = new[0].astype(bf16)
        grad = jnp.concatenate([grads[MELS], grads[MELS + 1]], 0)
        new = step_tile(grad, *(x[...] for x in ins[3:]), biases_rate)
        for ref, value in zip(held[4:], new):
            ref[...] = value
        held[7][...] = new[0].astype(bf16)
        copies = [
            pltpu.make_async_copy(a, b, sem.at[i]) for i, (a, b) in enumerate(zip(held, outs))
        ]
        for copy in copies:
            copy.start()
        return copies

    def update(key, items):
        trio, rate = matrices[key]
        n = len(items)

        def start(*refs):
            gs, trio_refs, outs = refs[:n], refs[n : n + 3], refs[n + 3 : n + 7]
            held, sem = refs[n + 7 : n + 11], refs[n + 11]
            copies = []
            for i, (total, k, lead) in enumerate(items):
                first = pl.multiple_of(total.pairs.quarter(k) * QUARTER, QUARTER)
                parts = [x if lead is None else x.at[lead] for x in (*trio_refs, *outs)]
                for r in range(0, QUARTER, 16):
                    span = slice(i * QUARTER + r, i * QUARTER + r + 16)
                    there = pl.ds(first + r, 16)
                    for c in range(0, GATE, 128):
                        w = slice(c, c + 128)
                        tile = r + c // 128
                        g = jnp.concatenate([gs[i][tile], gs[i][tile + 8]], 0)
                        new = step_tile(g, *(x[there, w] for x in parts[:3]), rate)
                        for ref, value in zip(held, new):
                            ref[span, w] = value
                        held[3][span, w] = new[0].astype(bf16)
                for o in range(4):
                    copies.append(
                        pltpu.make_async_copy(
                            held[o].at[pl.ds(i * QUARTER, QUARTER)],
                            parts[3 + o].at[pl.ds(first, QUARTER)],
                            sem.at[i * 4 + o],
                        )
                    )
                    copies[-1].start()
            return copies

        return Part(
            f"u{n}", [total.pieces[k] for total, k, _ in items] + [*trio],
            [(trio[0].shape, t) for t in kinds], start,
            lambda result: state.update({key: result}), old=state.get(key, ()),
            scratch=[pltpu.VMEM((n * QUARTER, GATE), t) for t in kinds]
            + [pltpu.SemaphoreType.DMA((4 * n,))],
        )

    def few_update():
        def start(*refs):
            return update_few(refs[:4], refs[4:10], refs[10:18], refs[18:26], refs[26], refs[27])

        return Part(
            "few", [*sums["1"].pieces, *few_args], few_shapes, start,
            lambda result: state.update(few=result),
            scratch=[pltpu.VMEM(*x) for x in few_shapes]
            + [pltpu.VMEM((96, 8, 128), f32), pltpu.SemaphoreType.DMA((8,))],
        )

    def spread(key):
        total = sums[key]
        while not total.done:
            total.advance()
        total.pieces = [total.piece, total.pairs.swap(total.piece, 0), total.pairs.swap(total.piece, 1)]

    def relay(key):
        total = sums[key]
        total.pieces.append(total.pairs.swap(total.pieces[2], 0))

    owners = {"P": ("proj", None), "0": ("conv", 0), "1": ("conv", 1)}
    fill = {"back": back}
    for i in range(2):
        fill[f"mix{i}"] = lambda i=i: mix(i * HALF)
        fill[f"sg{i}"] = lambda i=i: signal_grad(i * HALF)

    def updates(word):
        named = {}
        for letter in word[1:]:
            if letter in owners:
                key, lead = owners[letter]
                total = sums[letter]
            elif letter in "abcd":
                named.setdefault(key, []).append((total, "abcd".index(letter), lead))
        return [update(key, items) for key, items in named.items()] + (
            [few_update()] if "f" in word else []
        )

    for word in SCRIPT:
        if word in owners:
            sums[word].advance()
        elif word == "gg":
            gate_grad()
        elif len(word) == 2 and word[0] in "jksr":
            {"j": first_half, "k": second_half, "s": spread, "r": relay}[word[0]](word[1])
        else:
            work = []
            for item in word.split("+"):
                work += updates(item) if item[0] == "=" else [fill[item]()]
            run_parts(order, work)
    proj_new, conv_new = state["proj"], state["conv"]
    cond_new, bias_new = state["few"][:4], [x.reshape(-1) for x in state["few"][4:]]
    result = [*state["mixed"], *state["signal_grad"]]
    for k in range(4):
        result += [conv_new[k], cond_new[k], proj_new[k], bias_new[k]]
    return tuple(result)


WHOLE = (2, 1, 1)
SCRIPT = (
    "jP", "gg", "kP", "P", "j0", "k0", "j1", "k1", "P", "0", "sg0", "P", "1", "back", "0", "mix0",
    "P", "1", "mix1", "0", "1", "P", "0", "1", "0", "P", "1", "0", "sP", "rP", "sg1", "1", "0",
    "s0", "1", "s1", "=Pb", "r0", "=0abPacd", "r1", "=1a", "=0cd1bc", "=1df",
)


def shards(*args):
    return solve(Pairs("proj"), args)


def solution(mesh):
    rows = P(("blk", "seq"), None)
    in_specs = (rows, P(("blk", "seq")), P(("blk", "seq")), rows, rows, rows) + (P(),) * 12
    out_specs = (rows,) * 4 + (P(),) * 16
    return jax.shard_map(shards, mesh=mesh, in_specs=in_specs, out_specs=out_specs, check_vma=False)
```
